32 devices in a mesh: chan: 4 (over y, core), row: 8 (over z, x).
Axes of the slice: x: 2, y: 2, z: 4, core: 2. Of those that a mesh axis runs over, the one named last changes fastest.
Arguments:
- voltages: bfloat16 [64, 2, 4, 1024], P('row', None, 'chan'), may hold values from -6 to 6
- kernels: float32 [64, 2, 4], P('row'), may hold values from 0.1 to 1.9
- footprint: int32 [64, 2], P('row'), may hold values from 0 to 252
- cal_weight: float32 [8, 4], P(None, 'chan'), may hold values from -6 to 6
Outputs:
- power_image: float32 [4, 256, 256], P('chan', None, 'row')
- calibrator_maps: float32 [8, 256, 256], P('chan', None, 'row')
The draws below stay inside these ranges and needn't reach their ends.
All inputs are finite; a program needn't handle non-finite values.
Results may differ from the reference program's by a relative error of at most 0.004.
Values may be sent and summed in bfloat16 or wider, within the bound.
A program may use at most 256 MiB of HBM per device.

```python
import math
import jax
import jax.numpy as jnp
from jax import lax

GRID = 256
KW = 4
S_DEV = 8
NT = 1024
S = 64
CH = 4
Q = 8
ROW_DEV = 32


def draw_footprint(key, part):
    blocks = S // S_DEV
    key_base, key_offsets, key_columns = jax.random.split(jax.random.fold_in(key, 17), 3)
    base = jax.random.randint(key_base, (blocks, 1), 0, blocks - 6)
    base = base.at[0, 0].set(0)
    base = base.at[blocks - 1, 0].set(blocks - 7)
    pairs = jnp.arange(S_DEV, dtype=jnp.int32) // 2
    home = base + 2 * pairs[None, :]
    offsets = jax.random.randint(key_offsets, (blocks, S_DEV), 0, ROW_DEV)
    offsets = offsets.at[:, 1].set(ROW_DEV - 1)
    offsets = offsets.at[0, 0].set(0)
    offsets = offsets.at[blocks - 1, S_DEV - 1].set(ROW_DEV - 1)
    rows_first = jnp.minimum(home * ROW_DEV + offsets, GRID - KW)
    columns_first = jax.random.randint(key_columns, (blocks, S_DEV), 0, GRID - KW + 1)
    columns_first = columns_first.at[0, 0].set(0)
    columns_first = columns_first.at[0, 2].set(GRID - KW)
    return jnp.stack([rows_first.reshape(S), columns_first.reshape(S)], axis=1).astype(jnp.int32)


def shard_levels(stream_key, extent, pieces, smallest, largest):
    level, own = 1.0, jax.random.fold_in(stream_key, 6)
    for position, blocks in pieces:
        steps = jnp.exp(jax.random.uniform(jax.random.fold_in(own, position), (blocks,), jnp.float32, smallest / len(pieces), largest / len(pieces)))
        level = level * jnp.repeat(steps, extent[position] // blocks).reshape([-1 if axis == position else 1 for axis in range(len(extent))])
    return level


def centred(rng, extent, deviation, reach, cuts=(), kind=jnp.bfloat16):
    level = shard_levels(rng, extent, cuts, -0.22, 0.18) if cuts else 1.0
    entries = jax.random.normal(rng, extent, jnp.float32) * deviation * level
    return jnp.minimum(jnp.maximum(entries, -reach), reach).astype(kind)


def setup_inputs(seed: int = 0) -> dict:
    key_list = jax.random.split(jax.random.key(seed), 5)
    return {
        "voltages": centred(key_list[0], (S, 2, CH, NT), 1.0, 6.0, ((0, 8), (2, 4))),
        "kernels": jnp.clip(1.0 + 0.18 * jax.random.normal(key_list[1], (S, 2, KW), jnp.float32), 0.1, 1.9),
        "footprint": draw_footprint(jax.random.fold_in(key_list[4], 71), 0),
        "cal_weight": centred(key_list[3], (Q, CH), 1.0, 6.0, ((1, 4),), jnp.float32),
    }


def dft_tables(size, first, count):
    indices = jnp.arange(size, dtype=jnp.int32)
    columns = first + jnp.arange(count, dtype=jnp.int32)
    phases = (indices[:, None] * columns[None, :]) % size
    angles = phases.astype(jnp.float32) * (2.0 * math.pi / size)
    return jnp.cos(angles), jnp.sin(angles)


def placed(weights, starts, first, count):
    positions = first + jnp.arange(count, dtype=jnp.int32)
    taps = jnp.arange(weights.shape[1], dtype=jnp.int32)
    target = starts[:, None] + taps[None, :]
    hit = positions[None, None, :] == target[:, :, None]
    return jnp.sum(jnp.where(hit, weights[:, :, None], jnp.zeros((), weights.dtype)), axis=1)


def blocked_time_sum(values):
    samples = values.shape[-1]
    width = math.gcd(samples, 128)
    shaped = values.reshape(values.shape[:-1] + (samples // width, width))
    return jnp.sum(jnp.sum(shaped, axis=-1), axis=-1)


def reference(voltages, kernels, footprint, cal_weight):
    highest = lax.Precision.HIGHEST
    row_weight = placed(kernels[:, 0, :], footprint[:, 0], 0, GRID)
    col_weight = placed(kernels[:, 1, :], footprint[:, 1], 0, GRID)
    cos_table, sin_table = dft_tables(GRID, 0, GRID)
    power_scale = 1.0 / (2.0 * NT * S * KW * KW)
    by_channel = jnp.moveaxis(voltages.astype(jnp.float32), 2, 0)

    def one_channel(volt_block):
        volt_real = volt_block[:, 0, :]
        volt_imag = volt_block[:, 1, :]
        spread_real = row_weight.T[:, :, None] * volt_real[None, :, :]
        spread_imag = row_weight.T[:, :, None] * volt_imag[None, :, :]
        grid_real = jnp.einsum('ust,sv->uvt', spread_real, col_weight, precision=highest)
        grid_imag = jnp.einsum('ust,sv->uvt', spread_imag, col_weight, precision=highest)
        half_real = (jnp.einsum('uvt,vm->umt', grid_real, cos_table, precision=highest)
                     + jnp.einsum('uvt,vm->umt', grid_imag, sin_table, precision=highest))
        half_imag = (jnp.einsum('uvt,vm->umt', grid_imag, cos_table, precision=highest)
                     - jnp.einsum('uvt,vm->umt', grid_real, sin_table, precision=highest))
        sky_real = (jnp.einsum('umt,ul->lmt', half_real, cos_table, precision=highest)
                    + jnp.einsum('umt,ul->lmt', half_imag, sin_table, precision=highest))
        sky_imag = (jnp.einsum('umt,ul->lmt', half_imag, cos_table, precision=highest)
                    - jnp.einsum('umt,ul->lmt', half_real, sin_table, precision=highest))
        return blocked_time_sum(sky_real * sky_real + sky_imag * sky_imag) * power_scale

    power_image = lax.map(one_channel, by_channel)
    calibrator_maps = jnp.einsum('qc,clm->qlm', cal_weight, power_image, precision=highest)
    return power_image, calibrator_maps
```

```python
import functools
import math

import jax
import jax.numpy as jnp
from jax import lax
from jax.experimental import pallas as pl
from jax.experimental.pallas import tpu as pltpu
from jax.sharding import PartitionSpec as P

GRID = 256
HALVES = 2
LANES = 128
MESH = pl.DeviceIdType.MESH


def unit_circle(phase):
    turn = jnp.where(phase >= GRID // 2, phase - GRID, phase).astype(jnp.float32)
    half = turn * (math.pi / GRID)
    square = half * half
    sin_half = 0.0
    for order in (11, 9, 7, 5, 3, 1):
        sin_half = sin_half * square + (-1.0) ** (order // 2) / math.factorial(order)
    sin_half = sin_half * half
    cos_half = 0.0
    for order in (12, 10, 8, 6, 4, 2, 0):
        cos_half = cos_half * square + (-1.0) ** (order // 2) / math.factorial(order)
    return 1.0 - 2.0 * sin_half * sin_half, 2.0 * sin_half * cos_half


def response(weights, start, first, count):
    stations, taps = weights.shape
    place = first + lax.broadcasted_iota(jnp.int32, (stations, count), 1)
    base_real, base_imag = unit_circle((start * place) & (GRID - 1))
    step = lax.broadcasted_iota(jnp.int32, (8, count), 0)
    place = first + lax.broadcasted_iota(jnp.int32, (8, count), 1)
    tap_real, tap_imag = unit_circle((step * place) & (GRID - 1))
    sum_real, sum_imag = 0.0, 0.0
    for k in range(taps):
        weight = weights[:, k : k + 1]
        sum_real = sum_real + weight * tap_real[k : k + 1, :]
        sum_imag = sum_imag + weight * tap_imag[k : k + 1, :]
    return (
        base_real * sum_real - base_imag * sum_imag,
        base_real * sum_imag + base_imag * sum_real,
    )


def turned(values, local):
    lanes = values.shape[1]
    lane = lax.broadcasted_iota(jnp.int32, values.shape, 1)
    later = pltpu.roll(values, lanes - local, 1)
    earlier = pltpu.roll(values, local, 1)
    return jnp.where((lane // local) % 2 == 0, -later, earlier)


def gather_kernel(
    rows, chans, volt_ref, kern_ref, foot_ref, cal_ref,
    forms_ref, a_ref, b_ref,
    fields, meta, halves, held, visible,
    meta_send, meta_recv, volt_send, volt_recv, vis_send, vis_recv,
):
    row, chan = lax.axis_index("row"), lax.axis_index("chan")
    local = volt_ref.shape[0] // 2
    width = halves.shape[2]
    maps, taps = cal_ref.shape[1], kern_ref.shape[1]
    twin = row + 1 - 2 * (row % 2)
    row_peers = [(k, (row + k) % rows) for k in range(1, rows)]
    vis_peers = [
        (2 * d + h, (chan + d) % chans, twin if h else row)
        for d in range(chans) for h in range(2) if d or h
    ]

    barrier = pltpu.get_barrier_semaphore()
    for _, peer in row_peers:
        pl.semaphore_signal(barrier, inc=1, device_id={"chan": chan, "row": peer}, device_id_type=MESH)
    for k, other, peer in vis_peers:
        if k != 1:
            pl.semaphore_signal(barrier, inc=1, device_id={"chan": other, "row": peer}, device_id_type=MESH)

    fields[...] = jnp.zeros_like(fields)
    fields[0:taps, 0:local] = kern_ref[0]
    fields[taps : 2 * taps, 0:local] = kern_ref[1]
    fields[2 * taps : 2 * taps + 2, 0:local] = foot_ref[...].astype(jnp.float32)
    fields[2 * taps + 2 : 2 * taps + 3, 0:maps] = cal_ref[...]
    turned_fields = fields[...].T
    meta[row] = turned_fields[0:local, :]
    cal_column = turned_fields[0:maps, 2 * taps + 2 : 2 * taps + 3]
    for h in range(HALVES):
        halves[h] = volt_ref[:, h * width : (h + 1) * width]
    held[row] = halves[row % 2]

    pl.semaphore_wait(barrier, len(row_peers) + len(vis_peers) - 1)

    copies = []
    for k, peer in row_peers:
        copies.append(pltpu.make_async_remote_copy(
            src_ref=meta.at[row], dst_ref=meta.at[row],
            send_sem=meta_send.at[k], recv_sem=meta_recv.at[k],
            device_id={"chan": chan, "row": peer}, device_id_type=MESH,
        ))
        copies[-1].start()
    volt_copies = []
    for k, peer in row_peers:
        volt_copies.append(pltpu.make_async_remote_copy(
            src_ref=halves.at[peer % 2], dst_ref=held.at[row],
            send_sem=volt_send.at[k], recv_sem=volt_recv.at[k],
            device_id={"chan": chan, "row": peer}, device_id_type=MESH,
        ))
        volt_copies[-1].start()

    for copy in copies:
        copy.wait()
    stations = rows * local
    known = meta[...].reshape(stations, LANES)
    starts = known[:, 2 * taps : 2 * taps + 2].astype(jnp.int32)
    a_real, a_imag = response(known[:, 0:taps], starts[:, 0:1], 0, GRID)
    a_ref[0] = a_real
    a_ref[1] = a_imag
    b_real, b_imag = response(known[:, taps : 2 * taps], starts[:, 1:2], row * (GRID // rows), LANES)
    b_ref[0] = b_real
    b_ref[1] = b_imag

    for copy in volt_copies:
        copy.wait()
    both = 2 * stations
    volts = held[...].reshape(both, width)
    products = lax.dot_general(
        volts, volts, (((1,), (1,)), ((), ())), preferred_element_type=jnp.float32
    ).reshape(rows, 2, local, both)
    seen = products[:, 0].reshape(stations, both) - turned(products[:, 1].reshape(stations, both), local)
    mine = 2 * chan + row % 2
    visible[mine, 0:stations, :] = seen
    visible[mine, stations : stations + maps, :] = jnp.broadcast_to(cal_column, (maps, both))

    vis_copies = []
    for k, other, peer in vis_peers:
        vis_copies.append(pltpu.make_async_remote_copy(
            src_ref=visible.at[mine], dst_ref=visible.at[mine],
            send_sem=vis_send.at[k], recv_sem=vis_recv.at[k],
            device_id={"chan": other, "row": peer}, device_id_type=MESH,
        ))
        vis_copies[-1].start()
    for copy in vis_copies:
        copy.wait()

    forms_ref[0] = visible[2 * chan, 0:stations, :] + visible[2 * chan + 1, 0:stations, :]
    share = maps // chans
    sums = [0.0] * share
    for c in range(chans):
        total = visible[2 * c, 0:stations, :] + visible[2 * c + 1, 0:stations, :]
        for q in range(share):
            weight = visible[2 * c, pl.ds(stations + chan * share + q, 1), :]
            sums[q] = sums[q] + weight * total
    for q in range(share):
        forms_ref[1 + q] = sums[q]


def image_kernel(local, scale, forms_ref, a_ref, b_ref, power_ref, maps_ref, split):
    forms, stations, both = forms_ref.shape
    columns = power_ref.shape[1]
    devices = stations // local

    def laced(first, second):
        shape = (devices, local, first.shape[-1])
        return jnp.stack([first.reshape(shape), second.reshape(shape)], axis=1).reshape(both, first.shape[-1])

    for f in range(forms):
        top = forms_ref[f]
        whole = laced(top, turned(top, local))
        high = whole.astype(jnp.bfloat16)
        split[f * both : (f + 1) * both, 0:both] = high
        split[f * both : (f + 1) * both, both : 2 * both] = (whole - high.astype(jnp.float32)).astype(jnp.bfloat16)

    a_real, a_imag = a_ref[0], a_ref[1]
    for m in range(columns):
        b_real, b_imag = b_ref[0, :, m : m + 1], b_ref[1, :, m : m + 1]
        steer = laced(a_real * b_real - a_imag * b_imag, a_real * b_imag + a_imag * b_real)
        high = steer.astype(jnp.bfloat16)
        left = 2.0 * steer - high.astype(jnp.float32)
        right = jnp.dot(split[...], jnp.concatenate([high, high], axis=0), preferred_element_type=jnp.float32)
        for f in range(forms):
            line = jnp.sum(left * right[f * both : (f + 1) * both], axis=0, keepdims=True) * scale
            if f == 0:
                power_ref[0, m : m + 1, :] = line
            else:
                maps_ref[f - 1, m : m + 1, :] = line


def on_device(voltages, kernels, footprint, cal_weight):
    local, _, _, samples = voltages.shape
    rows, chans = lax.axis_size("row"), lax.axis_size("chan")
    taps, maps = kernels.shape[2], cal_weight.shape[0]
    stations = local * rows
    both = 2 * stations
    share = maps // chans
    columns = GRID // rows
    scale = 1.0 / (2.0 * samples * stations * taps * taps)
    volts = jnp.swapaxes(voltages[:, :, 0, :], 0, 1).reshape(2 * local, samples)
    vmem = pl.BlockSpec(memory_space=pltpu.VMEM)
    f32 = jnp.float32
    forms, a_table, b_table = pl.pallas_call(
        functools.partial(gather_kernel, rows, chans),
        out_shape=(
            jax.ShapeDtypeStruct((1 + share, stations, both), f32),
            jax.ShapeDtypeStruct((2, stations, GRID), f32),
            jax.ShapeDtypeStruct((2, stations, LANES), f32),
        ),
        in_specs=[vmem] * 4,
        out_specs=(vmem,) * 3,
        scratch_shapes=[
            pltpu.VMEM((LANES, LANES), f32),
            pltpu.VMEM((rows, local, LANES), f32),
            pltpu.VMEM((HALVES, 2 * local, samples // HALVES), jnp.bfloat16),
            pltpu.VMEM((rows, 2 * local, samples // HALVES), jnp.bfloat16),
            pltpu.VMEM((2 * chans, stations + maps, both), f32),
            pltpu.SemaphoreType.DMA((rows,)),
            pltpu.SemaphoreType.DMA((rows,)),
            pltpu.SemaphoreType.DMA((rows,)),
            pltpu.SemaphoreType.DMA((rows,)),
            pltpu.SemaphoreType.DMA((2 * chans,)),
            pltpu.SemaphoreType.DMA((2 * chans,)),
        ],
        compiler_params=pltpu.CompilerParams(
            collective_id=0, has_side_effects=True, vmem_limit_bytes=48 * 1024 * 1024
        ),
    )(volts, jnp.transpose(kernels, (1, 2, 0)), footprint.T, cal_weight.T)
    power, cal_maps = pl.pallas_call(
        functools.partial(image_kernel, local, scale),
        out_shape=(
            jax.ShapeDtypeStruct((1, columns, GRID), f32),
            jax.ShapeDtypeStruct((share, columns, GRID), f32),
        ),
        in_specs=[vmem] * 3,
        out_specs=(vmem,) * 2,
        scratch_shapes=[pltpu.VMEM(((1 + share) * both, 2 * both), jnp.bfloat16)],
        compiler_params=pltpu.CompilerParams(vmem_limit_bytes=48 * 1024 * 1024),
    )(forms, a_table, b_table)
    return jnp.swapaxes(power, 1, 2), jnp.swapaxes(cal_maps, 1, 2)


def solution(mesh):
    placed = (P("row", None, "chan", None), P("row", None, None), P("row", None), P(None, "chan"))
    return jax.shard_map(
        on_device,
        mesh=mesh,
        in_specs=placed,
        out_specs=(P("chan", None, "row"), P("chan", None, "row")),
        check_vma=False,
    )
```

```python
import functools
import math

import jax
import jax.numpy as jnp
from jax import lax
from jax.experimental import pallas as pl
from jax.experimental.pallas import tpu as pltpu
from jax.sharding import PartitionSpec as P

GRID = 256
HALVES = 2
LANES = 128
MESH = pl.DeviceIdType.MESH


def unit_circle(phase):
    turn = jnp.where(phase >= GRID // 2, phase - GRID, phase).astype(jnp.float32)
    half = turn * (math.pi / GRID)
    square = half * half
    sin_half = 0.0
    for order in (11, 9, 7, 5, 3, 1):
        sin_half = sin_half * square + (-1.0) ** (order // 2) / math.factorial(order)
    sin_half = sin_half * half
    cos_half = 0.0
    for order in (12, 10, 8, 6, 4, 2, 0):
        cos_half = cos_half * square + (-1.0) ** (order // 2) / math.factorial(order)
    return 1.0 - 2.0 * sin_half * sin_half, 2.0 * sin_half * cos_half


def response(weights, start, first, count):
    stations, taps = weights.shape
    place = first + lax.broadcasted_iota(jnp.int32, (stations, count), 1)
    base_real, base_imag = unit_circle((start * place) & (GRID - 1))
    step = lax.broadcasted_iota(jnp.int32, (8, count), 0)
    place = first + lax.broadcasted_iota(jnp.int32, (8, count), 1)
    tap_real, tap_imag = unit_circle((step * place) & (GRID - 1))
    sum_real, sum_imag = 0.0, 0.0
    for k in range(taps):
        weight = weights[:, k : k + 1]
        sum_real = sum_real + weight * tap_real[k : k + 1, :]
        sum_imag = sum_imag + weight * tap_imag[k : k + 1, :]
    return (
        base_real * sum_real - base_imag * sum_imag,
        base_real * sum_imag + base_imag * sum_real,
    )


def turned(values, local):
    lanes = values.shape[1]
    lane = lax.broadcasted_iota(jnp.int32, values.shape, 1)
    later = pltpu.roll(values, lanes - local, 1)
    earlier = pltpu.roll(values, local, 1)
    return jnp.where((lane // local) % 2 == 0, -later, earlier)


def gather_kernel(
    rows, chans, volt_hbm, kern_hbm, foot_hbm, cal_hbm,
    forms_ref, a_ref, b_ref,
    volt, kern, foot, cal, fields, meta, halves, held, visible,
    load, meta_send, meta_recv, volt_send, volt_recv, vis_send, vis_recv,
):
    row, chan = lax.axis_index("row"), lax.axis_index("chan")
    local = volt.shape[0]
    width = halves.shape[2]
    maps, taps = cal.shape[1], kern.shape[1]
    twin = row + 1 - 2 * (row % 2)
    row_peers = [(k, (row + k) % rows) for k in range(1, rows)]
    vis_peers = [
        (2 * d + h, (chan + d) % chans, twin if h else row)
        for d in range(chans) for h in range(2) if d or h
    ]

    barrier = pltpu.get_barrier_semaphore()
    for _, peer in row_peers:
        pl.semaphore_signal(barrier, inc=1, device_id={"chan": chan, "row": peer}, device_id_type=MESH)
    for k, other, peer in vis_peers:
        if k != 1:
            pl.semaphore_signal(barrier, inc=1, device_id={"chan": other, "row": peer}, device_id_type=MESH)

    loads = [
        pltpu.make_async_copy(source, target, load.at[k])
        for k, (source, target) in enumerate(
            ((kern_hbm, kern), (foot_hbm, foot), (cal_hbm, cal), (volt_hbm, volt))
        )
    ]
    for copy in loads:
        copy.start()
    fields[...] = jnp.zeros_like(fields)
    for copy in loads[:3]:
        copy.wait()
    fields[0:taps, 0:local] = kern[0]
    fields[taps : 2 * taps, 0:local] = kern[1]
    fields[2 * taps : 2 * taps + 2, 0:local] = foot[...].astype(jnp.float32)
    fields[2 * taps + 2 : 2 * taps + 3, 0:maps] = cal[...]
    turned_fields = fields[...].T
    meta[row] = turned_fields[0:local, :]
    cal_column = turned_fields[0:maps, 2 * taps + 2 : 2 * taps + 3]
    loads[3].wait()
    for h in range(HALVES):
        part = volt[:, :, h * width : (h + 1) * width].astype(jnp.float32)
        halves[h] = jnp.concatenate([part[:, 0, :], part[:, 1, :]], axis=0).astype(jnp.bfloat16)
    held[row] = halves[row % 2]

    pl.semaphore_wait(barrier, len(row_peers) + len(vis_peers) - 1)

    copies = []
    for k, peer in row_peers:
        copies.append(pltpu.make_async_remote_copy(
            src_ref=meta.at[row], dst_ref=meta.at[row],
            send_sem=meta_send.at[k], recv_sem=meta_recv.at[k],
            device_id={"chan": chan, "row": peer}, device_id_type=MESH,
        ))
        copies[-1].start()
    volt_copies = []
    for k, peer in row_peers:
        volt_copies.append(pltpu.make_async_remote_copy(
            src_ref=halves.at[peer % 2], dst_ref=held.at[row],
            send_sem=volt_send.at[k], recv_sem=volt_recv.at[k],
            device_id={"chan": chan, "row": peer}, device_id_type=MESH,
        ))
        volt_copies[-1].start()

    for copy in copies:
        copy.wait()
    stations = rows * local
    known = meta[...].reshape(stations, LANES)
    starts = known[:, 2 * taps : 2 * taps + 2].astype(jnp.int32)
    a_real, a_imag = response(known[:, 0:taps], starts[:, 0:1], 0, GRID)
    a_ref[0] = a_real
    a_ref[1] = a_imag
    b_real, b_imag = response(known[:, taps : 2 * taps], starts[:, 1:2], row * (GRID // rows), LANES)
    b_ref[0] = b_real
    b_ref[1] = b_imag

    for copy in volt_copies:
        copy.wait()
    both = 2 * stations
    volts = held[...].reshape(both, width)
    products = lax.dot_general(
        volts, volts, (((1,), (1,)), ((), ())), preferred_element_type=jnp.float32
    ).reshape(rows, 2, local, both)
    seen = products[:, 0].reshape(stations, both) - turned(products[:, 1].reshape(stations, both), local)
    mine = 2 * chan + row % 2
    half, kept = stations // 2, 3 * stations // 4
    visible[mine, 0:half, :] = seen[:half]
    visible[mine, half:kept, 0:stations] = seen[half:kept, stations:]
    visible[mine, half:kept, stations:both] = seen[kept:, stations:]
    visible[mine, kept : kept + maps, :] = jnp.broadcast_to(cal_column, (maps, both))

    vis_copies = []
    for k, other, peer in vis_peers:
        vis_copies.append(pltpu.make_async_remote_copy(
            src_ref=visible.at[mine], dst_ref=visible.at[mine],
            send_sem=vis_send.at[k], recv_sem=vis_recv.at[k],
            device_id={"chan": other, "row": peer}, device_id_type=MESH,
        ))
        vis_copies[-1].start()
    for copy in vis_copies:
        copy.wait()

    forms_ref[0] = visible[2 * chan, 0:kept, :] + visible[2 * chan + 1, 0:kept, :]
    share = maps // chans
    sums = [0.0] * share
    for c in range(chans):
        total = visible[2 * c, 0:kept, :] + visible[2 * c + 1, 0:kept, :]
        for q in range(share):
            weight = visible[2 * c, pl.ds(kept + chan * share + q, 1), :]
            sums[q] = sums[q] + weight * total
    for q in range(share):
        forms_ref[1 + q] = sums[q]


def image_kernel(local, scale, forms_ref, a_ref, b_ref, power_ref, maps_ref, split):
    forms, kept, both = forms_ref.shape
    stations, half = both // 2, both // 4
    columns = power_ref.shape[1]
    devices = stations // local

    def laced(first, second):
        shape = (devices, local, first.shape[-1])
        return jnp.stack([first.reshape(shape), second.reshape(shape)], axis=1).reshape(both, first.shape[-1])

    for f in range(forms):
        lane = lax.broadcasted_iota(jnp.int32, (half, both), 1)
        upper = jnp.where(lane < stations, 0.5, 1.0) * forms_ref[f, 0:half, :]
        packed = 0.5 * forms_ref[f, half:kept, :]
        lower = jnp.concatenate([pltpu.roll(packed, stations, 1), packed], axis=0)
        top = jnp.concatenate([upper, jnp.where(lane < stations, 0.0, lower)], axis=0)
        whole = laced(top, turned(top, local))
        whole = whole + whole.T
        high = whole.astype(jnp.bfloat16)
        split[f * both : (f + 1) * both, 0:both] = high
        split[f * both : (f + 1) * both, both : 2 * both] = (whole - high.astype(jnp.float32)).astype(jnp.bfloat16)

    a_real, a_imag = a_ref[0], a_ref[1]
    for m in range(columns):
        b_real, b_imag = b_ref[0, :, m : m + 1], b_ref[1, :, m : m + 1]
        steer = laced(a_real * b_real - a_imag * b_imag, a_real * b_imag + a_imag * b_real)
        high = steer.astype(jnp.bfloat16)
        left = 2.0 * steer - high.astype(jnp.float32)
        right = jnp.dot(split[...], jnp.concatenate([high, high], axis=0), preferred_element_type=jnp.float32)
        for f in range(forms):
            line = jnp.sum(left * right[f * both : (f + 1) * both], axis=0, keepdims=True) * scale
            if f == 0:
                power_ref[0, m : m + 1, :] = line
            else:
                maps_ref[f - 1, m : m + 1, :] = line


def on_device(voltages, kernels, footprint, cal_weight):
    local, _, _, samples = voltages.shape
    rows, chans = lax.axis_size("row"), lax.axis_size("chan")
    taps, maps = kernels.shape[2], cal_weight.shape[0]
    stations = local * rows
    both = 2 * stations
    share = maps // chans
    columns = GRID // rows
    scale = 1.0 / (2.0 * samples * stations * taps * taps)
    hbm = pl.BlockSpec(memory_space=pltpu.HBM)
    vmem = pl.BlockSpec(memory_space=pltpu.VMEM)
    f32 = jnp.float32
    forms, a_table, b_table = pl.pallas_call(
        functools.partial(gather_kernel, rows, chans),
        out_shape=(
            jax.ShapeDtypeStruct((1 + share, 3 * stations // 4, both), f32),
            jax.ShapeDtypeStruct((2, stations, GRID), f32),
            jax.ShapeDtypeStruct((2, stations, LANES), f32),
        ),
        in_specs=[hbm] * 4,
        out_specs=(vmem,) * 3,
        scratch_shapes=[
            pltpu.VMEM((local, 2, samples), jnp.bfloat16),
            pltpu.VMEM((2, taps, local), f32),
            pltpu.VMEM((2, local), jnp.int32),
            pltpu.VMEM((1, maps), f32),
            pltpu.VMEM((LANES, LANES), f32),
            pltpu.VMEM((rows, local, LANES), f32),
            pltpu.VMEM((HALVES, 2 * local, samples // HALVES), jnp.bfloat16),
            pltpu.VMEM((rows, 2 * local, samples // HALVES), jnp.bfloat16),
            pltpu.VMEM((2 * chans, 3 * stations // 4 + maps, both), f32),
            pltpu.SemaphoreType.DMA((4,)),
            pltpu.SemaphoreType.DMA((rows,)),
            pltpu.SemaphoreType.DMA((rows,)),
            pltpu.SemaphoreType.DMA((rows,)),
            pltpu.SemaphoreType.DMA((rows,)),
            pltpu.SemaphoreType.DMA((2 * chans,)),
            pltpu.SemaphoreType.DMA((2 * chans,)),
        ],
        compiler_params=pltpu.CompilerParams(
            collective_id=0, has_side_effects=True, vmem_limit_bytes=48 * 1024 * 1024
        ),
    )(*(
        pltpu.with_memory_space_constraint(x, pltpu.HBM)
        for x in (voltages[:, :, 0, :], jnp.transpose(kernels, (1, 2, 0)), footprint.T, cal_weight.T)
    ))
    power, cal_maps = pl.pallas_call(
        functools.partial(image_kernel, local, scale),
        out_shape=(
            jax.ShapeDtypeStruct((1, columns, GRID), f32),
            jax.ShapeDtypeStruct((share, columns, GRID), f32),
        ),
        in_specs=[vmem] * 3,
        out_specs=(vmem,) * 2,
        scratch_shapes=[pltpu.VMEM(((1 + share) * both, 2 * both), jnp.bfloat16)],
        compiler_params=pltpu.CompilerParams(vmem_limit_bytes=48 * 1024 * 1024),
    )(forms, a_table, b_table)
    return jnp.swapaxes(power, 1, 2), jnp.swapaxes(cal_maps, 1, 2)


def solution(mesh):
    placed = (P("row", None, "chan", None), P("row", None, None), P("row", None), P(None, "chan"))
    return jax.shard_map(
        on_device,
        mesh=mesh,
        in_specs=placed,
        out_specs=(P("chan", None, "row"), P("chan", None, "row")),
        check_vma=False,
    )
```

```python
import functools
import math

import jax
import jax.numpy as jnp
from jax import lax
from jax.experimental import pallas as pl
from jax.experimental.pallas import tpu as pltpu
from jax.sharding import PartitionSpec as P

GRID = 256
HALVES = 2
LANES = 128
MESH = pl.DeviceIdType.MESH


def unit_circle(phase):
    turn = jnp.where(phase >= GRID // 2, phase - GRID, phase).astype(jnp.float32)
    half = turn * (math.pi / GRID)
    square = half * half
    sin_half = 0.0
    for order in (11, 9, 7, 5, 3, 1):
        sin_half = sin_half * square + (-1.0) ** (order // 2) / math.factorial(order)
    sin_half = sin_half * half
    cos_half = 0.0
    for order in (12, 10, 8, 6, 4, 2, 0):
        cos_half = cos_half * square + (-1.0) ** (order // 2) / math.factorial(order)
    return 1.0 - 2.0 * sin_half * sin_half, 2.0 * sin_half * cos_half


def response(weights, start, first, count):
    stations, taps = weights.shape
    place = first + lax.broadcasted_iota(jnp.int32, (stations, count), 1)
    base_real, base_imag = unit_circle((start * place) & (GRID - 1))
    step = lax.broadcasted_iota(jnp.int32, (8, count), 0)
    place = first + lax.broadcasted_iota(jnp.int32, (8, count), 1)
    tap_real, tap_imag = unit_circle((step * place) & (GRID - 1))
    sum_real, sum_imag = 0.0, 0.0
    for k in range(taps):
        weight = weights[:, k : k + 1]
        sum_real = sum_real + weight * tap_real[k : k + 1, :]
        sum_imag = sum_imag + weight * tap_imag[k : k + 1, :]
    return (
        base_real * sum_real - base_imag * sum_imag,
        base_real * sum_imag + base_imag * sum_real,
    )


def turned(values, local):
    lanes = values.shape[1]
    lane = lax.broadcasted_iota(jnp.int32, values.shape, 1)
    later = pltpu.roll(values, lanes - local, 1)
    earlier = pltpu.roll(values, local, 1)
    return jnp.where((lane // local) % 2 == 0, -later, earlier)


def laced(first, second, local):
    shape = (first.shape[0] // local, local, first.shape[1])
    both = jnp.stack([first.reshape(shape), second.reshape(shape)], axis=1)
    return both.reshape(2 * first.shape[0], first.shape[1])


def gather_kernel(
    rows, chans, volt_hbm, kern_hbm, foot_hbm, cal_hbm,
    forms_ref, high_ref, left_ref,
    volt, kern, foot, cal, fields, meta, halves, held, visible,
    load, meta_send, meta_recv, volt_send, volt_recv, vis_send, vis_recv,
):
    row, chan = lax.axis_index("row"), lax.axis_index("chan")
    local = volt.shape[0]
    width = halves.shape[2]
    maps, taps = cal.shape[1], kern.shape[1]
    twin = row + 1 - 2 * (row % 2)
    row_peers = [(k, (row + k) % rows) for k in range(1, rows)]
    vis_peers = [
        (2 * d + h, (chan + d) % chans, twin if h else row)
        for d in range(chans) for h in range(2) if d or h
    ]

    barrier = pltpu.get_barrier_semaphore()
    for _, peer in row_peers:
        pl.semaphore_signal(barrier, inc=1, device_id={"chan": chan, "row": peer}, device_id_type=MESH)
    for k, other, peer in vis_peers:
        if k != 1:
            pl.semaphore_signal(barrier, inc=1, device_id={"chan": other, "row": peer}, device_id_type=MESH)

    loads = [
        pltpu.make_async_copy(source, target, load.at[k])
        for k, (source, target) in enumerate(
            ((volt_hbm, volt), (kern_hbm, kern), (foot_hbm, foot), (cal_hbm, cal))
        )
    ]
    for copy in loads:
        copy.start()
    loads[0].wait()
    for h in range(HALVES):
        part = volt[:, :, h * width : (h + 1) * width].astype(jnp.float32)
        halves[h] = jnp.concatenate([part[:, 0, :], part[:, 1, :]], axis=0).astype(jnp.bfloat16)
    held[row] = halves[row % 2]

    pl.semaphore_wait(barrier, len(row_peers) + len(vis_peers) - 1)

    volt_copies = []
    for k, peer in row_peers:
        volt_copies.append(pltpu.make_async_remote_copy(
            src_ref=halves.at[peer % 2], dst_ref=held.at[row],
            send_sem=volt_send.at[k], recv_sem=volt_recv.at[k],
            device_id={"chan": chan, "row": peer}, device_id_type=MESH,
        ))
        volt_copies[-1].start()

    fields[...] = jnp.zeros_like(fields)
    for copy in loads[1:]:
        copy.wait()
    fields[0:taps, 0:local] = kern[0]
    fields[taps : 2 * taps, 0:local] = kern[1]
    fields[2 * taps : 2 * taps + 2, 0:local] = foot[...].astype(jnp.float32)
    fields[2 * taps + 2 : 2 * taps + 3, 0:maps] = cal[...]
    turned_fields = fields[...].T
    meta[row] = turned_fields[0:local, :]
    cal_column = turned_fields[0:maps, 2 * taps + 2 : 2 * taps + 3]
    copies = []
    for k, peer in row_peers:
        copies.append(pltpu.make_async_remote_copy(
            src_ref=meta.at[row], dst_ref=meta.at[row],
            send_sem=meta_send.at[k], recv_sem=meta_recv.at[k],
            device_id={"chan": chan, "row": peer}, device_id_type=MESH,
        ))
        copies[-1].start()
    stations = rows * local
    for copy in volt_copies:
        copy.wait()
    both = 2 * stations
    volts = held[...].reshape(both, width)
    products = lax.dot_general(
        volts, volts, (((1,), (1,)), ((), ())), preferred_element_type=jnp.float32
    ).reshape(rows, 2, local, both)
    seen = products[:, 0].reshape(stations, both) - turned(products[:, 1].reshape(stations, both), local)
    mine = 2 * chan + row % 2
    half, kept = stations // 2, 3 * stations // 4
    visible[mine, 0:half, :] = seen[:half]
    visible[mine, half:kept, 0:stations] = seen[half:kept, stations:]
    visible[mine, half:kept, stations:both] = seen[kept:, stations:]
    visible[mine, kept : kept + maps, :] = jnp.broadcast_to(cal_column, (maps, both))

    vis_copies = []
    for k, other, peer in vis_peers:
        vis_copies.append(pltpu.make_async_remote_copy(
            src_ref=visible.at[mine], dst_ref=visible.at[mine],
            send_sem=vis_send.at[k], recv_sem=vis_recv.at[k],
            device_id={"chan": other, "row": peer}, device_id_type=MESH,
        ))
        vis_copies[-1].start()
    for copy in copies:
        copy.wait()
    known = meta[...].reshape(stations, LANES)
    starts = known[:, 2 * taps : 2 * taps + 2].astype(jnp.int32)
    a_real, a_imag = response(known[:, 0:taps], starts[:, 0:1], 0, GRID)
    b_real, b_imag = response(known[:, taps : 2 * taps], starts[:, 1:2], row * (GRID // rows), LANES)
    columns = left_ref.shape[0]
    group = min(columns, 4)

    def steer(step, carry):
        b_real, b_imag = carry
        for j in range(group):
            one_real, one_imag = b_real[:, j : j + 1], b_imag[:, j : j + 1]
            whole = laced(a_real * one_real - a_imag * one_imag, a_real * one_imag + a_imag * one_real, local)
            high = whole.astype(jnp.bfloat16)
            high_ref[step * group + j] = high
            left_ref[step * group + j] = 2.0 * whole - high.astype(jnp.float32)
        return pltpu.roll(b_real, LANES - group, 1), pltpu.roll(b_imag, LANES - group, 1)

    lax.fori_loop(0, columns // group, steer, (b_real, b_imag))

    for copy in vis_copies:
        copy.wait()

    forms_ref[0] = visible[2 * chan, 0:kept, :] + visible[2 * chan + 1, 0:kept, :]
    share = maps // chans
    sums = [0.0] * share
    for c in range(chans):
        total = visible[2 * c, 0:kept, :] + visible[2 * c + 1, 0:kept, :]
        for q in range(share):
            weight = visible[2 * c, pl.ds(kept + chan * share + q, 1), :]
            sums[q] = sums[q] + weight * total
    for q in range(share):
        forms_ref[1 + q] = sums[q]


def image_kernel(local, scale, forms_ref, high_ref, left_ref, power_ref, maps_ref, split):
    forms, kept, both = forms_ref.shape
    stations, half = both // 2, both // 4
    columns = power_ref.shape[1]

    for f in range(forms):
        lane = lax.broadcasted_iota(jnp.int32, (half, both), 1)
        upper = jnp.where(lane < stations, 0.5, 1.0) * forms_ref[f, 0:half, :]
        packed = 0.5 * forms_ref[f, half:kept, :]
        lower = jnp.concatenate([pltpu.roll(packed, stations, 1), packed], axis=0)
        top = jnp.concatenate([upper, jnp.where(lane < stations, 0.0, lower)], axis=0)
        whole = laced(top, turned(top, local), local)
        whole = whole + whole.T
        high = whole.astype(jnp.bfloat16)
        split[f * both : (f + 1) * both, 0:both] = high
        split[f * both : (f + 1) * both, both : 2 * both] = (whole - high.astype(jnp.float32)).astype(jnp.bfloat16)

    for m in range(columns):
        high, left = high_ref[m], left_ref[m]
        right = jnp.dot(split[...], jnp.concatenate([high, high], axis=0), preferred_element_type=jnp.float32)
        for f in range(forms):
            line = jnp.sum(left * right[f * both : (f + 1) * both], axis=0, keepdims=True) * scale
            if f == 0:
                power_ref[0, m : m + 1, :] = line
            else:
                maps_ref[f - 1, m : m + 1, :] = line


def on_device(voltages, kernels, footprint, cal_weight):
    local, _, _, samples = voltages.shape
    rows, chans = lax.axis_size("row"), lax.axis_size("chan")
    taps, maps = kernels.shape[2], cal_weight.shape[0]
    stations = local * rows
    both = 2 * stations
    share = maps // chans
    columns = GRID // rows
    scale = 1.0 / (2.0 * samples * stations * taps * taps)
    hbm = pl.BlockSpec(memory_space=pltpu.HBM)
    vmem = pl.BlockSpec(memory_space=pltpu.VMEM)
    f32 = jnp.float32
    forms, high, left = pl.pallas_call(
        functools.partial(gather_kernel, rows, chans),
        out_shape=(
            jax.ShapeDtypeStruct((1 + share, 3 * stations // 4, both), f32),
            jax.ShapeDtypeStruct((columns, both, GRID), jnp.bfloat16),
            jax.ShapeDtypeStruct((columns, both, GRID), f32),
        ),
        in_specs=[hbm] * 4,
        out_specs=(vmem,) * 3,
        scratch_shapes=[
            pltpu.VMEM((local, 2, samples), jnp.bfloat16),
            pltpu.VMEM((2, taps, local), f32),
            pltpu.VMEM((2, local), jnp.int32),
            pltpu.VMEM((1, maps), f32),
            pltpu.VMEM((LANES, LANES), f32),
            pltpu.VMEM((rows, local, LANES), f32),
            pltpu.VMEM((HALVES, 2 * local, samples // HALVES), jnp.bfloat16),
            pltpu.VMEM((rows, 2 * local, samples // HALVES), jnp.bfloat16),
            pltpu.VMEM((2 * chans, 3 * stations // 4 + maps, both), f32),
            pltpu.SemaphoreType.DMA((4,)),
            pltpu.SemaphoreType.DMA((rows,)),
            pltpu.SemaphoreType.DMA((rows,)),
            pltpu.SemaphoreType.DMA((rows,)),
            pltpu.SemaphoreType.DMA((rows,)),
            pltpu.SemaphoreType.DMA((2 * chans,)),
            pltpu.SemaphoreType.DMA((2 * chans,)),
        ],
        compiler_params=pltpu.CompilerParams(
            collective_id=0, has_side_effects=True, vmem_limit_bytes=20 * 1024 * 1024
        ),
    )(*(
        pltpu.with_memory_space_constraint(x, pltpu.HBM)
        for x in (voltages[:, :, 0, :], jnp.transpose(kernels, (1, 2, 0)), footprint.T, cal_weight.T)
    ))
    power, cal_maps = pl.pallas_call(
        functools.partial(image_kernel, local, scale),
        out_shape=(
            jax.ShapeDtypeStruct((1, columns, GRID), f32),
            jax.ShapeDtypeStruct((share, columns, GRID), f32),
        ),
        in_specs=[vmem] * 3,
        out_specs=(vmem,) * 2,
        scratch_shapes=[pltpu.VMEM(((1 + share) * both, 2 * both), jnp.bfloat16)],
        compiler_params=pltpu.CompilerParams(vmem_limit_bytes=20 * 1024 * 1024),
    )(forms, high, left)
    return jnp.swapaxes(power, 1, 2), jnp.swapaxes(cal_maps, 1, 2)


def solution(mesh):
    placed = (P("row", None, "chan", None), P("row", None, None), P("row", None), P(None, "chan"))
    return jax.shard_map(
        on_device,
        mesh=mesh,
        in_specs=placed,
        out_specs=(P("chan", None, "row"), P("chan", None, "row")),
        check_vma=False,
    )
```

```python
import functools
import math

import jax
import jax.numpy as jnp
from jax import lax
from jax.experimental import pallas as pl
from jax.experimental.pallas import tpu as pltpu
from jax.sharding import PartitionSpec as P

GRID = 256
HALVES = 2
LANES = 128
MESH = pl.DeviceIdType.MESH


def unit_circle(phase):
    turn = jnp.where(phase >= GRID // 2, phase - GRID, phase).astype(jnp.float32)
    half = turn * (math.pi / GRID)
    square = half * half
    sin_half = 0.0
    for order in (11, 9, 7, 5, 3, 1):
        sin_half = sin_half * square + (-1.0) ** (order // 2) / math.factorial(order)
    sin_half = sin_half * half
    cos_half = 0.0
    for order in (12, 10, 8, 6, 4, 2, 0):
        cos_half = cos_half * square + (-1.0) ** (order // 2) / math.factorial(order)
    return 1.0 - 2.0 * sin_half * sin_half, 2.0 * sin_half * cos_half


def response(weights, start, first, count):
    stations, taps = weights.shape
    place = first + lax.broadcasted_iota(jnp.int32, (stations, count), 1)
    base_real, base_imag = unit_circle((start * place) & (GRID - 1))
    step = lax.broadcasted_iota(jnp.int32, (8, count), 0)
    place = first + lax.broadcasted_iota(jnp.int32, (8, count), 1)
    tap_real, tap_imag = unit_circle((step * place) & (GRID - 1))
    sum_real, sum_imag = 0.0, 0.0
    for k in range(taps):
        weight = weights[:, k : k + 1]
        sum_real = sum_real + weight * tap_real[k : k + 1, :]
        sum_imag = sum_imag + weight * tap_imag[k : k + 1, :]
    return (
        base_real * sum_real - base_imag * sum_imag,
        base_real * sum_imag + base_imag * sum_real,
    )


def turned(values, local):
    lanes = values.shape[1]
    lane = lax.broadcasted_iota(jnp.int32, values.shape, 1)
    later = pltpu.roll(values, lanes - local, 1)
    earlier = pltpu.roll(values, local, 1)
    return jnp.where((lane // local) % 2 == 0, -later, earlier)


def laced(first, second, local):
    shape = (first.shape[0] // local, local, first.shape[1])
    both = jnp.stack([first.reshape(shape), second.reshape(shape)], axis=1)
    return both.reshape(2 * first.shape[0], first.shape[1])


def gather_kernel(
    rows, chans, volt_hbm, kern_hbm, foot_hbm, cal_hbm,
    forms_ref, high_ref, left_ref,
    volt, kern, foot, cal, fields, meta, halves, held, vis_near, vis_far,
    load, meta_send, meta_recv, volt_send, volt_recv, near_send, near_recv, far_send, far_recv,
):
    row, chan = lax.axis_index("row"), lax.axis_index("chan")
    local = volt.shape[0]
    width = halves.shape[2]
    maps, taps = cal.shape[1], kern.shape[1]
    twin = row + 1 - 2 * (row % 2)
    side = rows // 2
    mine_side, place = row // side, row % side
    row_peers = [(side, (1 - mine_side) * side + place)]
    for j in range(1, side):
        row_peers.append((j, mine_side * side + (place + j) % side))
        row_peers.append((side + j, (1 - mine_side) * side + (place + j) % side))
    slot = (row + mine_side * side) % rows
    vis_peers = [
        (2 * d + h, (chan + d) % chans, twin if h else row)
        for d in range(chans) for h in range(2) if d or h
    ]

    barrier = pltpu.get_barrier_semaphore()
    for _, peer in row_peers:
        pl.semaphore_signal(barrier, inc=1, device_id={"chan": chan, "row": peer}, device_id_type=MESH)
    for k, other, peer in vis_peers:
        if k != 1:
            pl.semaphore_signal(barrier, inc=1, device_id={"chan": other, "row": peer}, device_id_type=MESH)

    loads = [
        pltpu.make_async_copy(source, target, load.at[k])
        for k, (source, target) in enumerate(
            ((volt_hbm, volt), (kern_hbm, kern), (foot_hbm, foot), (cal_hbm, cal))
        )
    ]
    for copy in loads:
        copy.start()
    loads[0].wait()
    for h in range(HALVES):
        part = volt[:, :, h * width : (h + 1) * width].astype(jnp.float32)
        halves[h] = jnp.concatenate([part[:, 0, :], part[:, 1, :]], axis=0).astype(jnp.bfloat16)
    held[slot] = halves[row % 2]

    pl.semaphore_wait(barrier, len(row_peers) + len(vis_peers) - 1)

    volt_copies = []
    for k, peer in row_peers:
        volt_copies.append(pltpu.make_async_remote_copy(
            src_ref=halves.at[peer % 2], dst_ref=held.at[(row + peer // side * side) % rows],
            send_sem=volt_send.at[k], recv_sem=volt_recv.at[k],
            device_id={"chan": chan, "row": peer}, device_id_type=MESH,
        ))
        volt_copies[-1].start()

    fields[...] = jnp.zeros_like(fields)
    for copy in loads[1:]:
        copy.wait()
    fields[0:taps, 0:local] = kern[0]
    fields[taps : 2 * taps, 0:local] = kern[1]
    fields[2 * taps : 2 * taps + 2, 0:local] = foot[...].astype(jnp.float32)
    fields[2 * taps + 2 : 2 * taps + 3, 0:maps] = cal[...]
    turned_fields = fields[...].T
    meta[slot] = turned_fields[0:local, :]
    cal_column = turned_fields[0:maps, 2 * taps + 2 : 2 * taps + 3]
    copies = []
    for k, peer in row_peers:
        copies.append(pltpu.make_async_remote_copy(
            src_ref=meta.at[slot], dst_ref=meta.at[(row + peer // side * side) % rows],
            send_sem=meta_send.at[k], recv_sem=meta_recv.at[k],
            device_id={"chan": chan, "row": peer}, device_id_type=MESH,
        ))
        copies[-1].start()
    stations = rows * local
    both, quarter = 2 * stations, stations // 4
    mine = 2 * chan + row % 2

    def correlate(first, second):
        products = lax.dot_general(
            first, second, (((1,), (1,)), ((), ())), preferred_element_type=jnp.float32
        ).reshape(first.shape[0] // (2 * local), 2, local, both)
        count = first.shape[0] // 2
        return products[:, 0].reshape(count, both) - turned(products[:, 1].reshape(count, both), local)

    def exchange(buffer, send_sem, recv_sem):
        sends = []
        for k, other, peer in vis_peers:
            sends.append(pltpu.make_async_remote_copy(
                src_ref=buffer.at[mine], dst_ref=buffer.at[mine],
                send_sem=send_sem.at[k], recv_sem=recv_sem.at[k],
                device_id={"chan": other, "row": peer}, device_id_type=MESH,
            ))
            sends[-1].start()
        return sends

    left_lanes = lax.broadcasted_iota(jnp.int32, (quarter, both), 1) < stations
    for (k, _), copy in zip(row_peers, volt_copies):
        if k < side:
            copy.wait_recv()
    near = held[0:side].reshape(stations, width)
    seen = correlate(near, jnp.concatenate([near, near], axis=0))
    vis_near[mine, 0:quarter, :] = jnp.where(left_lanes, seen[:quarter], seen[quarter:])
    vis_near[mine, quarter : quarter + maps, :] = jnp.broadcast_to(cal_column, (maps, both))
    vis_copies = exchange(vis_near, near_send, near_recv)

    for (k, _), copy in zip(row_peers, volt_copies):
        if k >= side:
            copy.wait_recv()
    far = held[side:rows].reshape(stations, width)
    seen = correlate(jnp.concatenate([near, far], axis=0), jnp.concatenate([far, far], axis=0))
    for part in range(2):
        lo = 2 * part * quarter
        vis_far[mine, part * quarter : (part + 1) * quarter, :] = jnp.where(
            left_lanes, seen[lo : lo + quarter], seen[lo + quarter : lo + 2 * quarter]
        )
    vis_copies += exchange(vis_far, far_send, far_recv)
    for copy in copies:
        copy.wait()
    known = meta[...].reshape(stations, LANES)
    starts = known[:, 2 * taps : 2 * taps + 2].astype(jnp.int32)
    a_real, a_imag = response(known[:, 0:taps], starts[:, 0:1], 0, GRID)
    b_real, b_imag = response(known[:, taps : 2 * taps], starts[:, 1:2], row * (GRID // rows), LANES)
    columns = left_ref.shape[0]
    group = min(columns, 4)

    def steer(step, carry):
        b_real, b_imag = carry
        for j in range(group):
            one_real, one_imag = b_real[:, j : j + 1], b_imag[:, j : j + 1]
            whole = laced(a_real * one_real - a_imag * one_imag, a_real * one_imag + a_imag * one_real, local)
            high = whole.astype(jnp.bfloat16)
            high_ref[step * group + j] = high
            left_ref[step * group + j] = 2.0 * whole - high.astype(jnp.float32)
        return pltpu.roll(b_real, LANES - group, 1), pltpu.roll(b_imag, LANES - group, 1)

    lax.fori_loop(0, columns // group, steer, (b_real, b_imag))

    for copy in vis_copies:
        copy.wait()

    for copy in volt_copies:
        copy.wait_send()

    share = maps // chans
    near_total = [vis_near[2 * c, 0:quarter, :] + vis_near[2 * c + 1, 0:quarter, :] for c in range(chans)]
    far_total = [vis_far[2 * c] + vis_far[2 * c + 1] for c in range(chans)]
    forms_ref[0, 0:quarter, :] = vis_near[2 * chan, 0:quarter, :] + vis_near[2 * chan + 1, 0:quarter, :]
    forms_ref[0, quarter : 3 * quarter, :] = vis_far[2 * chan] + vis_far[2 * chan + 1]
    for q in range(share):
        near_sum, far_sum = 0.0, 0.0
        for c in range(chans):
            weight = vis_near[2 * c, pl.ds(quarter + chan * share + q, 1), :]
            near_sum = near_sum + weight * near_total[c]
            far_sum = far_sum + weight * far_total[c]
        forms_ref[1 + q, 0:quarter, :] = near_sum
        forms_ref[1 + q, quarter : 3 * quarter, :] = far_sum


def image_kernel(local, scale, forms_ref, high_ref, left_ref, power_ref, maps_ref, split):
    forms, _, both = forms_ref.shape
    stations, quarter = both // 2, both // 8
    columns = power_ref.shape[1]

    for f in range(forms):
        left_lanes = lax.broadcasted_iota(jnp.int32, (quarter, both), 1) < stations
        near, cross, far = (forms_ref[f, k * quarter : (k + 1) * quarter, :] for k in range(3))
        near, far = 0.5 * near, 0.5 * far
        top = jnp.concatenate([
            jnp.where(left_lanes, near, pltpu.roll(cross, stations, 1)),
            jnp.where(left_lanes, pltpu.roll(near, stations, 1), cross),
            jnp.where(left_lanes, 0.0, pltpu.roll(far, stations, 1)),
            jnp.where(left_lanes, 0.0, far),
        ], axis=0)
        whole = laced(top, turned(top, local), local)
        whole = whole + whole.T
        high = whole.astype(jnp.bfloat16)
        split[f * both : (f + 1) * both, 0:both] = high
        split[f * both : (f + 1) * both, both : 2 * both] = (whole - high.astype(jnp.float32)).astype(jnp.bfloat16)

    for m in range(columns):
        high, left = high_ref[m], left_ref[m]
        right = jnp.dot(split[...], jnp.concatenate([high, high], axis=0), preferred_element_type=jnp.float32)
        for f in range(forms):
            line = jnp.sum(left * right[f * both : (f + 1) * both], axis=0, keepdims=True) * scale
            if f == 0:
                power_ref[0, m : m + 1, :] = line
            else:
                maps_ref[f - 1, m : m + 1, :] = line


def on_device(voltages, kernels, footprint, cal_weight):
    local, _, _, samples = voltages.shape
    rows, chans = lax.axis_size("row"), lax.axis_size("chan")
    taps, maps = kernels.shape[2], cal_weight.shape[0]
    stations = local * rows
    both = 2 * stations
    share = maps // chans
    columns = GRID // rows
    scale = 1.0 / (2.0 * samples * stations * taps * taps)
    hbm = pl.BlockSpec(memory_space=pltpu.HBM)
    vmem = pl.BlockSpec(memory_space=pltpu.VMEM)
    f32 = jnp.float32
    forms, high, left = pl.pallas_call(
        functools.partial(gather_kernel, rows, chans),
        out_shape=(
            jax.ShapeDtypeStruct((1 + share, 3 * stations // 4, both), f32),
            jax.ShapeDtypeStruct((columns, both, GRID), jnp.bfloat16),
            jax.ShapeDtypeStruct((columns, both, GRID), f32),
        ),
        in_specs=[hbm] * 4,
        out_specs=(vmem,) * 3,
        scratch_shapes=[
            pltpu.VMEM((local, 2, samples), jnp.bfloat16),
            pltpu.VMEM((2, taps, local), f32),
            pltpu.VMEM((2, local), jnp.int32),
            pltpu.VMEM((1, maps), f32),
            pltpu.VMEM((LANES, LANES), f32),
            pltpu.VMEM((rows, local, LANES), f32),
            pltpu.VMEM((HALVES, 2 * local, samples // HALVES), jnp.bfloat16),
            pltpu.VMEM((rows, 2 * local, samples // HALVES), jnp.bfloat16),
            pltpu.VMEM((2 * chans, stations // 4 + maps, both), f32),
            pltpu.VMEM((2 * chans, stations // 2, both), f32),
            pltpu.SemaphoreType.DMA((4,)),
            pltpu.SemaphoreType.DMA((rows,)),
            pltpu.SemaphoreType.DMA((rows,)),
            pltpu.SemaphoreType.DMA((rows,)),
            pltpu.SemaphoreType.DMA((rows,)),
            pltpu.SemaphoreType.DMA((2 * chans,)),
            pltpu.SemaphoreType.DMA((2 * chans,)),
            pltpu.SemaphoreType.DMA((2 * chans,)),
            pltpu.SemaphoreType.DMA((2 * chans,)),
        ],
        compiler_params=pltpu.CompilerParams(
            collective_id=0, has_side_effects=True, vmem_limit_bytes=20 * 1024 * 1024
        ),
    )(*(
        pltpu.with_memory_space_constraint(x, pltpu.HBM)
        for x in (voltages[:, :, 0, :], jnp.transpose(kernels, (1, 2, 0)), footprint.T, cal_weight.T)
    ))
    power, cal_maps = pl.pallas_call(
        functools.partial(image_kernel, local, scale),
        out_shape=(
            jax.ShapeDtypeStruct((1, columns, GRID), f32),
            jax.ShapeDtypeStruct((share, columns, GRID), f32),
        ),
        in_specs=[vmem] * 3,
        out_specs=(vmem,) * 2,
        scratch_shapes=[pltpu.VMEM(((1 + share) * both, 2 * both), jnp.bfloat16)],
        compiler_params=pltpu.CompilerParams(vmem_limit_bytes=20 * 1024 * 1024),
    )(forms, high, left)
    return jnp.swapaxes(power, 1, 2), jnp.swapaxes(cal_maps, 1, 2)


def solution(mesh):
    placed = (P("row", None, "chan", None), P("row", None, None), P("row", None), P(None, "chan"))
    return jax.shard_map(
        on_device,
        mesh=mesh,
        in_specs=placed,
        out_specs=(P("chan", None, "row"), P("chan", None, "row")),
        check_vma=False,
    )
```

```python
import functools
import math

import jax
import jax.numpy as jnp
from jax import lax
from jax.experimental import pallas as pl
from jax.experimental.pallas import tpu as pltpu
from jax.sharding import PartitionSpec as P

GRID = 256
HALVES = 2
LANES = 128
MESH = pl.DeviceIdType.MESH


def unit_circle(phase):
    turn = jnp.where(phase >= GRID // 2, phase - GRID, phase).astype(jnp.float32)
    half = turn * (math.pi / GRID)
    square = half * half
    sin_half = 0.0
    for order in (11, 9, 7, 5, 3, 1):
        sin_half = sin_half * square + (-1.0) ** (order // 2) / math.factorial(order)
    sin_half = sin_half * half
    cos_half = 0.0
    for order in (12, 10, 8, 6, 4, 2, 0):
        cos_half = cos_half * square + (-1.0) ** (order // 2) / math.factorial(order)
    return 1.0 - 2.0 * sin_half * sin_half, 2.0 * sin_half * cos_half


def response(weights, start, first, count):
    stations, taps = weights.shape
    place = first + lax.broadcasted_iota(jnp.int32, (stations, count), 1)
    base_real, base_imag = unit_circle((start * place) & (GRID - 1))
    step = lax.broadcasted_iota(jnp.int32, (8, count), 0)
    place = first + lax.broadcasted_iota(jnp.int32, (8, count), 1)
    tap_real, tap_imag = unit_circle((step * place) & (GRID - 1))
    sum_real, sum_imag = 0.0, 0.0
    for k in range(taps):
        weight = weights[:, k : k + 1]
        sum_real = sum_real + weight * tap_real[k : k + 1, :]
        sum_imag = sum_imag + weight * tap_imag[k : k + 1, :]
    return (
        base_real * sum_real - base_imag * sum_imag,
        base_real * sum_imag + base_imag * sum_real,
    )


def turned(values, local):
    lanes = values.shape[1]
    lane = lax.broadcasted_iota(jnp.int32, values.shape, 1)
    later = pltpu.roll(values, lanes - local, 1)
    earlier = pltpu.roll(values, local, 1)
    return jnp.where((lane // local) % 2 == 0, -later, earlier)


def laced(first, second, local):
    shape = (first.shape[0] // local, local, first.shape[1])
    both = jnp.stack([first.reshape(shape), second.reshape(shape)], axis=1)
    return both.reshape(2 * first.shape[0], first.shape[1])


def symmetric(near, cross, far, local):
    quarter, both = near.shape
    stations = both // 2
    left_lanes = lax.broadcasted_iota(jnp.int32, (quarter, both), 1) < stations
    near, far = 0.5 * near, 0.5 * far
    top = jnp.concatenate([
        jnp.where(left_lanes, near, pltpu.roll(cross, stations, 1)),
        jnp.where(left_lanes, pltpu.roll(near, stations, 1), cross),
        jnp.where(left_lanes, 0.0, pltpu.roll(far, stations, 1)),
        jnp.where(left_lanes, 0.0, far),
    ], axis=0)
    whole = laced(top, turned(top, local), local)
    whole = whole + whole.T
    high = whole.astype(jnp.bfloat16)
    return high, (whole - high.astype(jnp.float32)).astype(jnp.bfloat16)


def gather_kernel(
    rows, chans, volt_hbm, kern_hbm, foot_hbm, cal_hbm,
    forms_ref, high_ref, left_ref, own_ref,
    volt, kern, foot, cal, fields, meta, halves, held, vis_near, vis_far, split,
    load, meta_send, meta_recv, volt_send, volt_recv, near_send, near_recv, far_send, far_recv,
):
    row, chan = lax.axis_index("row"), lax.axis_index("chan")
    local = volt.shape[0]
    width = halves.shape[2]
    maps, taps = cal.shape[1], kern.shape[1]
    twin = row + 1 - 2 * (row % 2)
    side = rows // 2
    mine_side, place = row // side, row % side
    row_peers = [(side, (1 - mine_side) * side + place)]
    for j in range(1, side):
        row_peers.append((j, mine_side * side + (place + j) % side))
        row_peers.append((side + j, (1 - mine_side) * side + (place + j) % side))
    slot = (row + mine_side * side) % rows
    vis_peers = [
        (2 * d + h, (chan + d) % chans, twin if h else row)
        for d in range(chans) for h in range(2) if d or h
    ]

    barrier = pltpu.get_barrier_semaphore()
    for _, peer in row_peers:
        pl.semaphore_signal(barrier, inc=1, device_id={"chan": chan, "row": peer}, device_id_type=MESH)
    for k, other, peer in vis_peers:
        if k != 1:
            pl.semaphore_signal(barrier, inc=1, device_id={"chan": other, "row": peer}, device_id_type=MESH)

    loads = [
        pltpu.make_async_copy(source, target, load.at[k])
        for k, (source, target) in enumerate(
            ((volt_hbm, volt), (kern_hbm, kern), (foot_hbm, foot), (cal_hbm, cal))
        )
    ]
    for copy in loads:
        copy.start()
    loads[0].wait()
    for h in range(HALVES):
        part = volt[:, :, h * width : (h + 1) * width].astype(jnp.float32)
        halves[h] = jnp.concatenate([part[:, 0, :], part[:, 1, :]], axis=0).astype(jnp.bfloat16)
    held[slot] = halves[row % 2]

    pl.semaphore_wait(barrier, len(row_peers) + len(vis_peers) - 1)

    volt_copies = []
    for k, peer in row_peers:
        volt_copies.append(pltpu.make_async_remote_copy(
            src_ref=halves.at[peer % 2], dst_ref=held.at[(row + peer // side * side) % rows],
            send_sem=volt_send.at[k], recv_sem=volt_recv.at[k],
            device_id={"chan": chan, "row": peer}, device_id_type=MESH,
        ))
        volt_copies[-1].start()

    fields[...] = jnp.zeros_like(fields)
    for copy in loads[1:]:
        copy.wait()
    fields[0:taps, 0:local] = kern[0]
    fields[taps : 2 * taps, 0:local] = kern[1]
    fields[2 * taps : 2 * taps + 2, 0:local] = foot[...].astype(jnp.float32)
    fields[2 * taps + 2 : 2 * taps + 3, 0:maps] = cal[...]
    turned_fields = fields[...].T
    meta[slot] = turned_fields[0:local, :]
    cal_column = turned_fields[0:maps, 2 * taps + 2 : 2 * taps + 3]
    copies = []
    for k, peer in row_peers:
        copies.append(pltpu.make_async_remote_copy(
            src_ref=meta.at[slot], dst_ref=meta.at[(row + peer // side * side) % rows],
            send_sem=meta_send.at[k], recv_sem=meta_recv.at[k],
            device_id={"chan": chan, "row": peer}, device_id_type=MESH,
        ))
        copies[-1].start()
    stations = rows * local
    both, quarter = 2 * stations, stations // 4
    mine = 2 * chan + row % 2

    def correlate(first, second):
        products = lax.dot_general(
            first, second, (((1,), (1,)), ((), ())), preferred_element_type=jnp.float32
        ).reshape(first.shape[0] // (2 * local), 2, local, both)
        count = first.shape[0] // 2
        return products[:, 0].reshape(count, both) - turned(products[:, 1].reshape(count, both), local)

    def exchange(buffer, send_sem, recv_sem):
        sends = []
        for k, other, peer in vis_peers:
            sends.append(pltpu.make_async_remote_copy(
                src_ref=buffer.at[mine], dst_ref=buffer.at[mine],
                send_sem=send_sem.at[k], recv_sem=recv_sem.at[k],
                device_id={"chan": other, "row": peer}, device_id_type=MESH,
            ))
            sends[-1].start()
        return sends

    left_lanes = lax.broadcasted_iota(jnp.int32, (quarter, both), 1) < stations
    for (k, _), copy in zip(row_peers, volt_copies):
        if k < side:
            copy.wait_recv()
    near = held[0:side].reshape(stations, width)
    seen = correlate(near, jnp.concatenate([near, near], axis=0))
    vis_near[mine, 0:quarter, :] = jnp.where(left_lanes, seen[:quarter], seen[quarter:])
    vis_near[mine, quarter : quarter + maps, :] = jnp.broadcast_to(cal_column, (maps, both))
    vis_copies = exchange(vis_near, near_send, near_recv)

    for (k, _), copy in zip(row_peers, volt_copies):
        if k >= side:
            copy.wait_recv()
    far = held[side:rows].reshape(stations, width)
    seen = correlate(jnp.concatenate([near, far], axis=0), jnp.concatenate([far, far], axis=0))
    for part in range(2):
        lo = 2 * part * quarter
        vis_far[mine, part * quarter : (part + 1) * quarter, :] = jnp.where(
            left_lanes, seen[lo : lo + quarter], seen[lo + quarter : lo + 2 * quarter]
        )
    vis_copies += exchange(vis_far, far_send, far_recv)
    for copy in copies:
        copy.wait()
    known = meta[...].reshape(stations, LANES)
    starts = known[:, 2 * taps : 2 * taps + 2].astype(jnp.int32)
    a_real, a_imag = response(known[:, 0:taps], starts[:, 0:1], 0, GRID)
    b_real, b_imag = response(known[:, taps : 2 * taps], starts[:, 1:2], row * (GRID // rows), LANES)
    columns = left_ref.shape[0]
    group = min(columns, 4)

    def steer(step, carry):
        b_real, b_imag = carry
        for j in range(group):
            one_real, one_imag = b_real[:, j : j + 1], b_imag[:, j : j + 1]
            whole = laced(a_real * one_real - a_imag * one_imag, a_real * one_imag + a_imag * one_real, local)
            high = whole.astype(jnp.bfloat16)
            high_ref[step * group + j] = high
            left_ref[step * group + j] = 2.0 * whole - high.astype(jnp.float32)
        return pltpu.roll(b_real, LANES - group, 1), pltpu.roll(b_imag, LANES - group, 1)

    lax.fori_loop(0, columns // group, steer, (b_real, b_imag))

    for copy in (vis_copies[0], vis_copies[len(vis_peers)]):
        copy.wait_recv()
    own = vis_far[2 * chan] + vis_far[2 * chan + 1]
    high, low = symmetric(
        vis_near[2 * chan, 0:quarter, :] + vis_near[2 * chan + 1, 0:quarter, :],
        own[:quarter], own[quarter:], local,
    )
    split[:, 0:both] = high
    split[:, both : 2 * both] = low
    batch = min(columns, 8)

    def image(step, carry):
        lines = []
        for j in range(batch):
            one = high_ref[step * batch + j]
            right = jnp.dot(split[...], jnp.concatenate([one, one], axis=0), preferred_element_type=jnp.float32)
            lines.append(jnp.sum(left_ref[step * batch + j] * right, axis=0, keepdims=True))
        own_ref[pl.ds(pl.multiple_of(step * batch, batch), batch), :] = jnp.concatenate(lines, axis=0)
        return carry

    lax.fori_loop(0, columns // batch, image, 0)

    for k, copy in enumerate(vis_copies):
        copy.wait_send()
        if k % len(vis_peers):
            copy.wait_recv()
    for copy in volt_copies:
        copy.wait_send()

    share = maps // chans
    near_total = [vis_near[2 * c, 0:quarter, :] + vis_near[2 * c + 1, 0:quarter, :] for c in range(chans)]
    far_total = [vis_far[2 * c] + vis_far[2 * c + 1] for c in range(chans)]
    for q in range(share):
        near_sum, far_sum = 0.0, 0.0
        for c in range(chans):
            weight = vis_near[2 * c, pl.ds(quarter + chan * share + q, 1), :]
            near_sum = near_sum + weight * near_total[c]
            far_sum = far_sum + weight * far_total[c]
        forms_ref[q, 0:quarter, :] = near_sum
        forms_ref[q, quarter : 3 * quarter, :] = far_sum


def image_kernel(local, scale, forms_ref, high_ref, left_ref, own_ref, power_ref, maps_ref, split):
    power_ref[0] = own_ref[...] * scale
    forms, _, both = forms_ref.shape
    quarter = both // 8
    columns = power_ref.shape[1]

    for f in range(forms):
        parts = [forms_ref[f, k * quarter : (k + 1) * quarter, :] for k in range(3)]
        high, low = symmetric(*parts, local)
        split[f * both : (f + 1) * both, 0:both] = high
        split[f * both : (f + 1) * both, both : 2 * both] = low

    for m in range(columns):
        high, left = high_ref[m], left_ref[m]
        right = jnp.dot(split[...], jnp.concatenate([high, high], axis=0), preferred_element_type=jnp.float32)
        for f in range(forms):
            line = jnp.sum(left * right[f * both : (f + 1) * both], axis=0, keepdims=True) * scale
            maps_ref[f, m : m + 1, :] = line


def on_device(voltages, kernels, footprint, cal_weight):
    local, _, _, samples = voltages.shape
    rows, chans = lax.axis_size("row"), lax.axis_size("chan")
    taps, maps = kernels.shape[2], cal_weight.shape[0]
    stations = local * rows
    both = 2 * stations
    share = maps // chans
    columns = GRID // rows
    scale = 1.0 / (2.0 * samples * stations * taps * taps)
    hbm = pl.BlockSpec(memory_space=pltpu.HBM)
    vmem = pl.BlockSpec(memory_space=pltpu.VMEM)
    f32 = jnp.float32
    forms, high, left, own = pl.pallas_call(
        functools.partial(gather_kernel, rows, chans),
        out_shape=(
            jax.ShapeDtypeStruct((share, 3 * stations // 4, both), f32),
            jax.ShapeDtypeStruct((columns, both, GRID), jnp.bfloat16),
            jax.ShapeDtypeStruct((columns, both, GRID), f32),
            jax.ShapeDtypeStruct((columns, GRID), f32),
        ),
        in_specs=[hbm] * 4,
        out_specs=(vmem,) * 4,
        scratch_shapes=[
            pltpu.VMEM((local, 2, samples), jnp.bfloat16),
            pltpu.VMEM((2, taps, local), f32),
            pltpu.VMEM((2, local), jnp.int32),
            pltpu.VMEM((1, maps), f32),
            pltpu.VMEM((LANES, LANES), f32),
            pltpu.VMEM((rows, local, LANES), f32),
            pltpu.VMEM((HALVES, 2 * local, samples // HALVES), jnp.bfloat16),
            pltpu.VMEM((rows, 2 * local, samples // HALVES), jnp.bfloat16),
            pltpu.VMEM((2 * chans, stations // 4 + maps, both), f32),
            pltpu.VMEM((2 * chans, stations // 2, both), f32),
            pltpu.VMEM((both, 2 * both), jnp.bfloat16),
            pltpu.SemaphoreType.DMA((4,)),
            pltpu.SemaphoreType.DMA((rows,)),
            pltpu.SemaphoreType.DMA((rows,)),
            pltpu.SemaphoreType.DMA((rows,)),
            pltpu.SemaphoreType.DMA((rows,)),
            pltpu.SemaphoreType.DMA((2 * chans,)),
            pltpu.SemaphoreType.DMA((2 * chans,)),
            pltpu.SemaphoreType.DMA((2 * chans,)),
            pltpu.SemaphoreType.DMA((2 * chans,)),
        ],
        compiler_params=pltpu.CompilerParams(
            collective_id=0, has_side_effects=True, vmem_limit_bytes=20 * 1024 * 1024
        ),
    )(*(
        pltpu.with_memory_space_constraint(x, pltpu.HBM)
        for x in (voltages[:, :, 0, :], jnp.transpose(kernels, (1, 2, 0)), footprint.T, cal_weight.T)
    ))
    power, cal_maps = pl.pallas_call(
        functools.partial(image_kernel, local, scale),
        out_shape=(
            jax.ShapeDtypeStruct((1, columns, GRID), f32),
            jax.ShapeDtypeStruct((share, columns, GRID), f32),
        ),
        in_specs=[vmem] * 4,
        out_specs=(vmem,) * 2,
        scratch_shapes=[pltpu.VMEM((share * both, 2 * both), jnp.bfloat16)],
        compiler_params=pltpu.CompilerParams(vmem_limit_bytes=20 * 1024 * 1024),
    )(forms, high, left, own)
    return jnp.swapaxes(power, 1, 2), jnp.swapaxes(cal_maps, 1, 2)


def solution(mesh):
    placed = (P("row", None, "chan", None), P("row", None, None), P("row", None), P(None, "chan"))
    return jax.shard_map(
        on_device,
        mesh=mesh,
        in_specs=placed,
        out_specs=(P("chan", None, "row"), P("chan", None, "row")),
        check_vma=False,
    )
```

```python
import functools
import math

import jax
import jax.numpy as jnp
from jax import lax
from jax.experimental import pallas as pl
from jax.experimental.pallas import tpu as pltpu
from jax.sharding import PartitionSpec as P

GRID = 256
HALVES = 2
LANES = 128
MESH = pl.DeviceIdType.MESH


def unit_circle(phase):
    turn = jnp.where(phase >= GRID // 2, phase - GRID, phase).astype(jnp.float32)
    half = turn * (math.pi / GRID)
    square = half * half
    sin_half = 0.0
    for order in (11, 9, 7, 5, 3, 1):
        sin_half = sin_half * square + (-1.0) ** (order // 2) / math.factorial(order)
    sin_half = sin_half * half
    cos_half = 0.0
    for order in (12, 10, 8, 6, 4, 2, 0):
        cos_half = cos_half * square + (-1.0) ** (order // 2) / math.factorial(order)
    return 1.0 - 2.0 * sin_half * sin_half, 2.0 * sin_half * cos_half


def response(weights, start, first, count):
    stations, taps = weights.shape
    place = first + lax.broadcasted_iota(jnp.int32, (stations, count), 1)
    base_real, base_imag = unit_circle((start * place) & (GRID - 1))
    step = lax.broadcasted_iota(jnp.int32, (8, count), 0)
    place = first + lax.broadcasted_iota(jnp.int32, (8, count), 1)
    tap_real, tap_imag = unit_circle((step * place) & (GRID - 1))
    sum_real, sum_imag = 0.0, 0.0
    for k in range(taps):
        weight = weights[:, k : k + 1]
        sum_real = sum_real + weight * tap_real[k : k + 1, :]
        sum_imag = sum_imag + weight * tap_imag[k : k + 1, :]
    return (
        base_real * sum_real - base_imag * sum_imag,
        base_real * sum_imag + base_imag * sum_real,
    )


def turned(values, local):
    lanes = values.shape[1]
    lane = lax.broadcasted_iota(jnp.int32, values.shape, 1)
    later = pltpu.roll(values, lanes - local, 1)
    earlier = pltpu.roll(values, local, 1)
    return jnp.where((lane // local) % 2 == 0, -later, earlier)


def laced(first, second, local):
    shape = (first.shape[0] // local, local, first.shape[1])
    both = jnp.stack([first.reshape(shape), second.reshape(shape)], axis=1)
    return both.reshape(2 * first.shape[0], first.shape[1])


def symmetric(near, cross, far, local):
    quarter, both = near.shape
    stations = both // 2
    left_lanes = lax.broadcasted_iota(jnp.int32, (quarter, both), 1) < stations
    near, far = 0.5 * near, 0.5 * far
    top = jnp.concatenate([
        jnp.where(left_lanes, near, pltpu.roll(cross, stations, 1)),
        jnp.where(left_lanes, pltpu.roll(near, stations, 1), cross),
        jnp.where(left_lanes, 0.0, pltpu.roll(far, stations, 1)),
        jnp.where(left_lanes, 0.0, far),
    ], axis=0)
    whole = laced(top, turned(top, local), local)
    whole = whole + whole.T
    high = whole.astype(jnp.bfloat16)
    return high, (whole - high.astype(jnp.float32)).astype(jnp.bfloat16)


def gather_kernel(
    rows, chans, volt_hbm, kern_hbm, foot_hbm, cal_hbm,
    forms_ref, high_ref, left_ref, own_ref,
    volt, kern, foot, cal, fields, meta, halves, held, own_near, got_near, own_far, got_far, all_near, all_far, split,
    load, meta_send, meta_recv, volt_send, volt_recv, twin_send, twin_recv, near_send, near_recv, far_send, far_recv,
):
    row, chan = lax.axis_index("row"), lax.axis_index("chan")
    local = volt.shape[0]
    width = halves.shape[2]
    maps, taps = cal.shape[1], kern.shape[1]
    twin = row + 1 - 2 * (row % 2)
    side = rows // 2
    mine_side, place = row // side, row % side
    row_peers = [(side, (1 - mine_side) * side + place)]
    for j in range(1, side):
        row_peers.append((j, mine_side * side + (place + j) % side))
        row_peers.append((side + j, (1 - mine_side) * side + (place + j) % side))
    slot = (row + mine_side * side) % rows
    chan_peers = [(k, (chan + k) % chans) for k in range(1, chans)]

    barrier = pltpu.get_barrier_semaphore()
    for _, peer in row_peers:
        pl.semaphore_signal(barrier, inc=1, device_id={"chan": chan, "row": peer}, device_id_type=MESH)
    for _, peer in chan_peers:
        pl.semaphore_signal(barrier, inc=1, device_id={"chan": peer, "row": row}, device_id_type=MESH)

    loads = [
        pltpu.make_async_copy(source, target, load.at[k])
        for k, (source, target) in enumerate(
            ((volt_hbm, volt), (kern_hbm, kern), (foot_hbm, foot), (cal_hbm, cal))
        )
    ]
    for copy in loads:
        copy.start()
    fields[...] = jnp.zeros_like(fields)
    for copy in loads[1:]:
        copy.wait()
    fields[0:taps, 0:local] = kern[0]
    fields[taps : 2 * taps, 0:local] = kern[1]
    fields[2 * taps : 2 * taps + 2, 0:local] = foot[...].astype(jnp.float32)
    fields[2 * taps + 2 : 2 * taps + 3, 0:maps] = cal[...]
    turned_fields = fields[...].T
    meta[slot] = turned_fields[0:local, :]
    cal_column = turned_fields[0:maps, 2 * taps + 2 : 2 * taps + 3]
    loads[0].wait()
    for h in range(HALVES):
        part = volt[:, :, h * width : (h + 1) * width].astype(jnp.float32)
        halves[h] = jnp.concatenate([part[:, 0, :], part[:, 1, :]], axis=0).astype(jnp.bfloat16)
    held[slot] = halves[row % 2]

    pl.semaphore_wait(barrier, len(row_peers) + len(chan_peers))

    copies = []
    for k, peer in row_peers:
        copies.append(pltpu.make_async_remote_copy(
            src_ref=meta.at[slot], dst_ref=meta.at[(row + peer // side * side) % rows],
            send_sem=meta_send.at[k], recv_sem=meta_recv.at[k],
            device_id={"chan": chan, "row": peer}, device_id_type=MESH,
        ))
        copies[-1].start()
    volt_copies = []
    for k, peer in row_peers:
        volt_copies.append(pltpu.make_async_remote_copy(
            src_ref=halves.at[peer % 2], dst_ref=held.at[(row + peer // side * side) % rows],
            send_sem=volt_send.at[k], recv_sem=volt_recv.at[k],
            device_id={"chan": chan, "row": peer}, device_id_type=MESH,
        ))
        volt_copies[-1].start()

    stations = rows * local
    both, quarter = 2 * stations, stations // 4

    def correlate(first, second):
        products = lax.dot_general(
            first, second, (((1,), (1,)), ((), ())), preferred_element_type=jnp.float32
        ).reshape(first.shape[0] // (2 * local), 2, local, both)
        count = first.shape[0] // 2
        return products[:, 0].reshape(count, both) - turned(products[:, 1].reshape(count, both), local)

    sends = []

    def to_twin(k, source, target):
        copy = pltpu.make_async_remote_copy(
            src_ref=source, dst_ref=target, send_sem=twin_send.at[k], recv_sem=twin_recv.at[k],
            device_id={"chan": chan, "row": twin}, device_id_type=MESH,
        )
        copy.start()
        sends.append(copy)
        return copy

    def to_channels(buffer, send_sem, recv_sem):
        copies = []
        for k, peer in chan_peers:
            copies.append(pltpu.make_async_remote_copy(
                src_ref=buffer.at[chan], dst_ref=buffer.at[chan],
                send_sem=send_sem.at[k], recv_sem=recv_sem.at[k],
                device_id={"chan": peer, "row": row}, device_id_type=MESH,
            ))
            copies[-1].start()
        sends.extend(copies)
        return copies

    left_lanes = lax.broadcasted_iota(jnp.int32, (quarter, both), 1) < stations
    for (k, _), copy in zip(row_peers, volt_copies):
        if k < side:
            copy.wait_recv()
    near = held[0:side].reshape(stations, width)
    seen = correlate(near, jnp.concatenate([near, near], axis=0))
    own_near[...] = jnp.where(left_lanes, seen[:quarter], seen[quarter:])
    near_copy = to_twin(0, own_near, got_near)

    for copy in copies:
        copy.wait()
    known = meta[...].reshape(stations, LANES)
    starts = known[:, 2 * taps : 2 * taps + 2].astype(jnp.int32)
    a_real, a_imag = response(known[:, 0:taps], starts[:, 0:1], 0, GRID)
    b_real, b_imag = response(known[:, taps : 2 * taps], starts[:, 1:2], row * (GRID // rows), LANES)
    columns = left_ref.shape[0]
    group = min(columns, 4)

    def steer(step, carry):
        b_real, b_imag = carry
        for j in range(group):
            one_real, one_imag = b_real[:, j : j + 1], b_imag[:, j : j + 1]
            whole = laced(a_real * one_real - a_imag * one_imag, a_real * one_imag + a_imag * one_real, local)
            high = whole.astype(jnp.bfloat16)
            high_ref[step * group + j] = high
            left_ref[step * group + j] = 2.0 * whole - high.astype(jnp.float32)
        return pltpu.roll(b_real, LANES - group, 1), pltpu.roll(b_imag, LANES - group, 1)

    steps = columns // group
    carry = lax.fori_loop(0, steps // 2, steer, (b_real, b_imag))

    near_copy.wait_recv()
    all_near[chan, 0:quarter, :] = own_near[...] + got_near[...]
    all_near[chan, quarter : quarter + maps, :] = jnp.broadcast_to(cal_column, (maps, both))
    chan_copies = to_channels(all_near, near_send, near_recv)

    for (k, _), copy in zip(row_peers, volt_copies):
        if k >= side:
            copy.wait_recv()
    far = held[side:rows].reshape(stations, width)
    seen = correlate(jnp.concatenate([near, far], axis=0), jnp.concatenate([far, far], axis=0))
    for part in range(2):
        lo = 2 * part * quarter
        own_far[part * quarter : (part + 1) * quarter, :] = jnp.where(
            left_lanes, seen[lo : lo + quarter], seen[lo + quarter : lo + 2 * quarter]
        )
    far_copy = to_twin(1, own_far, got_far)

    lax.fori_loop(steps // 2, steps, steer, carry)

    far_copy.wait_recv()
    all_far[chan] = own_far[...] + got_far[...]
    chan_copies += to_channels(all_far, far_send, far_recv)

    high, low = symmetric(all_near[chan, 0:quarter, :], all_far[chan, 0:quarter, :], all_far[chan, quarter:, :], local)
    split[:, 0:both] = high
    split[:, both : 2 * both] = low
    batch = min(columns, 8)

    def image(step, carry):
        lines = []
        for j in range(batch):
            one = high_ref[step * batch + j]
            right = jnp.dot(split[...], jnp.concatenate([one, one], axis=0), preferred_element_type=jnp.float32)
            lines.append(jnp.sum(left_ref[step * batch + j] * right, axis=0, keepdims=True))
        own_ref[pl.ds(pl.multiple_of(step * batch, batch), batch), :] = jnp.concatenate(lines, axis=0)
        return carry

    lax.fori_loop(0, columns // batch, image, 0)

    for copy in chan_copies:
        copy.wait_recv()
    for copy in sends:
        copy.wait_send()
    for copy in volt_copies:
        copy.wait_send()

    share = maps // chans
    for q in range(share):
        near_sum, far_sum = 0.0, 0.0
        for c in range(chans):
            weight = all_near[c, pl.ds(quarter + chan * share + q, 1), :]
            near_sum = near_sum + weight * all_near[c, 0:quarter, :]
            far_sum = far_sum + weight * all_far[c]
        forms_ref[q, 0:quarter, :] = near_sum
        forms_ref[q, quarter : 3 * quarter, :] = far_sum


def image_kernel(local, scale, forms_ref, high_ref, left_ref, own_ref, power_ref, maps_ref, split):
    power_ref[0] = own_ref[...] * scale
    forms, _, both = forms_ref.shape
    quarter = both // 8
    columns = power_ref.shape[1]

    for f in range(forms):
        parts = [forms_ref[f, k * quarter : (k + 1) * quarter, :] for k in range(3)]
        high, low = symmetric(*parts, local)
        split[f * both : (f + 1) * both, 0:both] = high
        split[f * both : (f + 1) * both, both : 2 * both] = low

    for m in range(columns):
        high, left = high_ref[m], left_ref[m]
        right = jnp.dot(split[...], jnp.concatenate([high, high], axis=0), preferred_element_type=jnp.float32)
        for f in range(forms):
            line = jnp.sum(left * right[f * both : (f + 1) * both], axis=0, keepdims=True) * scale
            maps_ref[f, m : m + 1, :] = line


def on_device(voltages, kernels, footprint, cal_weight):
    local, _, _, samples = voltages.shape
    rows, chans = lax.axis_size("row"), lax.axis_size("chan")
    taps, maps = kernels.shape[2], cal_weight.shape[0]
    stations = local * rows
    both = 2 * stations
    share = maps // chans
    columns = GRID // rows
    scale = 1.0 / (2.0 * samples * stations * taps * taps)
    hbm = pl.BlockSpec(memory_space=pltpu.HBM)
    vmem = pl.BlockSpec(memory_space=pltpu.VMEM)
    f32 = jnp.float32
    forms, high, left, own = pl.pallas_call(
        functools.partial(gather_kernel, rows, chans),
        out_shape=(
            jax.ShapeDtypeStruct((share, 3 * stations // 4, both), f32),
            jax.ShapeDtypeStruct((columns, both, GRID), jnp.bfloat16),
            jax.ShapeDtypeStruct((columns, both, GRID), f32),
            jax.ShapeDtypeStruct((columns, GRID), f32),
        ),
        in_specs=[hbm] * 4,
        out_specs=(vmem,) * 4,
        scratch_shapes=[
            pltpu.VMEM((local, 2, samples), jnp.bfloat16),
            pltpu.VMEM((2, taps, local), f32),
            pltpu.VMEM((2, local), jnp.int32),
            pltpu.VMEM((1, maps), f32),
            pltpu.VMEM((LANES, LANES), f32),
            pltpu.VMEM((rows, local, LANES), f32),
            pltpu.VMEM((HALVES, 2 * local, samples // HALVES), jnp.bfloat16),
            pltpu.VMEM((rows, 2 * local, samples // HALVES), jnp.bfloat16),
            pltpu.VMEM((stations // 4, both), f32),
            pltpu.VMEM((stations // 4, both), f32),
            pltpu.VMEM((stations // 2, both), f32),
            pltpu.VMEM((stations // 2, both), f32),
            pltpu.VMEM((chans, stations // 4 + maps, both), f32),
            pltpu.VMEM((chans, stations // 2, both), f32),
            pltpu.VMEM((both, 2 * both), jnp.bfloat16),
            pltpu.SemaphoreType.DMA((4,)),
            pltpu.SemaphoreType.DMA((rows,)),
            pltpu.SemaphoreType.DMA((rows,)),
            pltpu.SemaphoreType.DMA((rows,)),
            pltpu.SemaphoreType.DMA((rows,)),
            pltpu.SemaphoreType.DMA((2,)),
            pltpu.SemaphoreType.DMA((2,)),
            pltpu.SemaphoreType.DMA((chans,)),
            pltpu.SemaphoreType.DMA((chans,)),
            pltpu.SemaphoreType.DMA((chans,)),
            pltpu.SemaphoreType.DMA((chans,)),
        ],
        compiler_params=pltpu.CompilerParams(
            collective_id=0, has_side_effects=True, vmem_limit_bytes=20 * 1024 * 1024
        ),
    )(*(
        pltpu.with_memory_space_constraint(x, pltpu.HBM)
        for x in (voltages[:, :, 0, :], jnp.transpose(kernels, (1, 2, 0)), footprint.T, cal_weight.T)
    ))
    power, cal_maps = pl.pallas_call(
        functools.partial(image_kernel, local, scale),
        out_shape=(
            jax.ShapeDtypeStruct((1, columns, GRID), f32),
            jax.ShapeDtypeStruct((share, columns, GRID), f32),
        ),
        in_specs=[vmem] * 4,
        out_specs=(vmem,) * 2,
        scratch_shapes=[pltpu.VMEM((share * both, 2 * both), jnp.bfloat16)],
        compiler_params=pltpu.CompilerParams(vmem_limit_bytes=20 * 1024 * 1024),
    )(forms, high, left, own)
    return jnp.swapaxes(power, 1, 2), jnp.swapaxes(cal_maps, 1, 2)


def solution(mesh):
    placed = (P("row", None, "chan", None), P("row", None, None), P("row", None), P(None, "chan"))
    return jax.shard_map(
        on_device,
        mesh=mesh,
        in_specs=placed,
        out_specs=(P("chan", None, "row"), P("chan", None, "row")),
        check_vma=False,
    )
```

```python
import functools
import math

import jax
import jax.numpy as jnp
from jax import lax
from jax.experimental import pallas as pl
from jax.experimental.pallas import tpu as pltpu
from jax.sharding import PartitionSpec as P

GRID = 256
HALVES = 2
LANES = 128
MESH = pl.DeviceIdType.MESH


def unit_circle(phase):
    turn = jnp.where(phase >= GRID // 2, phase - GRID, phase).astype(jnp.float32)
    half = turn * (math.pi / GRID)
    square = half * half
    sin_half = 0.0
    for order in (11, 9, 7, 5, 3, 1):
        sin_half = sin_half * square + (-1.0) ** (order // 2) / math.factorial(order)
    sin_half = sin_half * half
    cos_half = 0.0
    for order in (12, 10, 8, 6, 4, 2, 0):
        cos_half = cos_half * square + (-1.0) ** (order // 2) / math.factorial(order)
    return 1.0 - 2.0 * sin_half * sin_half, 2.0 * sin_half * cos_half


def response(weights, start, first, count):
    stations, taps = weights.shape
    place = first + lax.broadcasted_iota(jnp.int32, (stations, count), 1)
    base_real, base_imag = unit_circle((start * place) & (GRID - 1))
    step = lax.broadcasted_iota(jnp.int32, (8, count), 0)
    place = first + lax.broadcasted_iota(jnp.int32, (8, count), 1)
    tap_real, tap_imag = unit_circle((step * place) & (GRID - 1))
    sum_real, sum_imag = 0.0, 0.0
    for k in range(taps):
        weight = weights[:, k : k + 1]
        sum_real = sum_real + weight * tap_real[k : k + 1, :]
        sum_imag = sum_imag + weight * tap_imag[k : k + 1, :]
    return (
        base_real * sum_real - base_imag * sum_imag,
        base_real * sum_imag + base_imag * sum_real,
    )


def turned(values, local):
    lanes = values.shape[1]
    lane = lax.broadcasted_iota(jnp.int32, values.shape, 1)
    later = pltpu.roll(values, lanes - local, 1)
    earlier = pltpu.roll(values, local, 1)
    return jnp.where((lane // local) % 2 == 0, -later, earlier)


def laced(first, second, local):
    shape = (first.shape[0] // local, local, first.shape[1])
    both = jnp.stack([first.reshape(shape), second.reshape(shape)], axis=1)
    return both.reshape(2 * first.shape[0], first.shape[1])


def symmetric(near, cross, far, local):
    quarter, both = near.shape
    stations = both // 2
    left_lanes = lax.broadcasted_iota(jnp.int32, (quarter, both), 1) < stations
    near, far = 0.5 * near, 0.5 * far
    top = jnp.concatenate([
        jnp.where(left_lanes, near, pltpu.roll(cross, stations, 1)),
        jnp.where(left_lanes, pltpu.roll(near, stations, 1), cross),
        jnp.where(left_lanes, 0.0, pltpu.roll(far, stations, 1)),
        jnp.where(left_lanes, 0.0, far),
    ], axis=0)
    whole = laced(top, turned(top, local), local)
    whole = whole + whole.T
    high = whole.astype(jnp.bfloat16)
    return high, (whole - high.astype(jnp.float32)).astype(jnp.bfloat16)


def gather_kernel(
    rows, chans, volt_hbm, kern_hbm, foot_hbm, cal_hbm,
    forms_ref, high_ref, left_ref, own_ref,
    volt, kern, foot, cal, fields, meta, halves, held, own_near, got_near, own_far, got_far, all_near, all_far, split,
    load, meta_send, meta_recv, volt_send, volt_recv, twin_send, twin_recv, near_send, near_recv, far_send, far_recv,
):
    row, chan = lax.axis_index("row"), lax.axis_index("chan")
    local = volt.shape[0]
    width = halves.shape[2]
    maps, taps = cal.shape[1], kern.shape[1]
    twin = row + 1 - 2 * (row % 2)
    side = rows // 2
    mine_side, place = row // side, row % side
    row_peers = [(side, (1 - mine_side) * side + place)]
    for j in range(1, side):
        row_peers.append((j, mine_side * side + (place + j) % side))
        row_peers.append((side + j, (1 - mine_side) * side + (place + j) % side))
    slot = (row + mine_side * side) % rows
    chan_peers = [(k, (chan + k) % chans) for k in range(1, chans)]

    barrier = pltpu.get_barrier_semaphore()
    for _, peer in row_peers:
        pl.semaphore_signal(barrier, inc=1, device_id={"chan": chan, "row": peer}, device_id_type=MESH)
    for _, peer in chan_peers:
        pl.semaphore_signal(barrier, inc=1, device_id={"chan": peer, "row": row}, device_id_type=MESH)

    loads = [
        pltpu.make_async_copy(source, target, load.at[k])
        for k, (source, target) in enumerate(
            ((volt_hbm, volt), (kern_hbm, kern), (foot_hbm, foot), (cal_hbm, cal))
        )
    ]
    for copy in loads:
        copy.start()
    loads[0].wait()
    for h in range(HALVES):
        part = volt[:, :, h * width : (h + 1) * width].astype(jnp.float32)
        halves[h] = jnp.concatenate([part[:, 0, :], part[:, 1, :]], axis=0).astype(jnp.bfloat16)
    held[slot] = halves[row % 2]

    pl.semaphore_wait(barrier, len(row_peers) + len(chan_peers))

    volt_copies = []
    for k, peer in row_peers:
        volt_copies.append(pltpu.make_async_remote_copy(
            src_ref=halves.at[peer % 2], dst_ref=held.at[(row + peer // side * side) % rows],
            send_sem=volt_send.at[k], recv_sem=volt_recv.at[k],
            device_id={"chan": chan, "row": peer}, device_id_type=MESH,
        ))
        volt_copies[-1].start()

    fields[...] = jnp.zeros_like(fields)
    for copy in loads[1:]:
        copy.wait()
    fields[0:taps, 0:local] = kern[0]
    fields[taps : 2 * taps, 0:local] = kern[1]
    fields[2 * taps : 2 * taps + 2, 0:local] = foot[...].astype(jnp.float32)
    fields[2 * taps + 2 : 2 * taps + 3, 0:maps] = cal[...]
    turned_fields = fields[...].T
    meta[slot] = turned_fields[0:local, :]
    cal_column = turned_fields[0:maps, 2 * taps + 2 : 2 * taps + 3]
    copies = []
    for k, peer in row_peers:
        copies.append(pltpu.make_async_remote_copy(
            src_ref=meta.at[slot], dst_ref=meta.at[(row + peer // side * side) % rows],
            send_sem=meta_send.at[k], recv_sem=meta_recv.at[k],
            device_id={"chan": chan, "row": peer}, device_id_type=MESH,
        ))
        copies[-1].start()

    stations = rows * local
    both, quarter = 2 * stations, stations // 4

    def correlate(first, second):
        products = lax.dot_general(
            first, second, (((1,), (1,)), ((), ())), preferred_element_type=jnp.float32
        ).reshape(first.shape[0] // (2 * local), 2, local, both)
        count = first.shape[0] // 2
        return products[:, 0].reshape(count, both) - turned(products[:, 1].reshape(count, both), local)

    sends = []

    def to_twin(k, source, target):
        copy = pltpu.make_async_remote_copy(
            src_ref=source, dst_ref=target, send_sem=twin_send.at[k], recv_sem=twin_recv.at[k],
            device_id={"chan": chan, "row": twin}, device_id_type=MESH,
        )
        copy.start()
        sends.append(copy)
        return copy

    def to_channels(buffer, send_sem, recv_sem):
        copies = []
        for k, peer in chan_peers:
            copies.append(pltpu.make_async_remote_copy(
                src_ref=buffer.at[chan], dst_ref=buffer.at[chan],
                send_sem=send_sem.at[k], recv_sem=recv_sem.at[k],
                device_id={"chan": peer, "row": row}, device_id_type=MESH,
            ))
            copies[-1].start()
        sends.extend(copies)
        return copies

    left_lanes = lax.broadcasted_iota(jnp.int32, (quarter, both), 1) < stations
    for (k, _), copy in zip(row_peers, volt_copies):
        if k < side:
            copy.wait_recv()
    near = held[0:side].reshape(stations, width)
    seen = correlate(near, jnp.concatenate([near, near], axis=0))
    own_near[...] = jnp.where(left_lanes, seen[:quarter], seen[quarter:])
    near_copy = to_twin(0, own_near, got_near)

    for (k, _), copy in zip(row_peers, volt_copies):
        if k >= side:
            copy.wait_recv()
    far = held[side:rows].reshape(stations, width)
    seen = correlate(jnp.concatenate([near, far], axis=0), jnp.concatenate([far, far], axis=0))
    for part in range(2):
        lo = 2 * part * quarter
        own_far[part * quarter : (part + 1) * quarter, :] = jnp.where(
            left_lanes, seen[lo : lo + quarter], seen[lo + quarter : lo + 2 * quarter]
        )
    far_copy = to_twin(1, own_far, got_far)

    near_copy.wait_recv()
    all_near[chan, 0:quarter, :] = own_near[...] + got_near[...]
    all_near[chan, quarter : quarter + maps, :] = jnp.broadcast_to(cal_column, (maps, both))
    chan_copies = to_channels(all_near, near_send, near_recv)

    for copy in copies:
        copy.wait()
    known = meta[...].reshape(stations, LANES)
    starts = known[:, 2 * taps : 2 * taps + 2].astype(jnp.int32)
    a_real, a_imag = response(known[:, 0:taps], starts[:, 0:1], 0, GRID)
    b_real, b_imag = response(known[:, taps : 2 * taps], starts[:, 1:2], row * (GRID // rows), LANES)
    columns = left_ref.shape[0]
    group = min(columns, 4)

    def steer(step, carry):
        b_real, b_imag = carry
        for j in range(group):
            one_real, one_imag = b_real[:, j : j + 1], b_imag[:, j : j + 1]
            whole = laced(a_real * one_real - a_imag * one_imag, a_real * one_imag + a_imag * one_real, local)
            high = whole.astype(jnp.bfloat16)
            high_ref[step * group + j] = high
            left_ref[step * group + j] = 2.0 * whole - high.astype(jnp.float32)
        return pltpu.roll(b_real, LANES - group, 1), pltpu.roll(b_imag, LANES - group, 1)

    steps = columns // group
    carry = lax.fori_loop(0, steps // 4, steer, (b_real, b_imag))

    far_copy.wait_recv()
    all_far[chan] = own_far[...] + got_far[...]
    chan_copies += to_channels(all_far, far_send, far_recv)

    lax.fori_loop(steps // 4, steps, steer, carry)

    high, low = symmetric(all_near[chan, 0:quarter, :], all_far[chan, 0:quarter, :], all_far[chan, quarter:, :], local)
    split[:, 0:both] = high
    split[:, both : 2 * both] = low
    batch = min(columns, 8)

    def image(step, carry):
        lines = []
        for j in range(batch):
            one = high_ref[step * batch + j]
            right = jnp.dot(split[...], jnp.concatenate([one, one], axis=0), preferred_element_type=jnp.float32)
            lines.append(jnp.sum(left_ref[step * batch + j] * right, axis=0, keepdims=True))
        own_ref[pl.ds(pl.multiple_of(step * batch, batch), batch), :] = jnp.concatenate(lines, axis=0)
        return carry

    lax.fori_loop(0, columns // batch, image, 0)

    for copy in sends + volt_copies:
        copy.wait_send()

    share = maps // chans
    for copy in chan_copies[: chans - 1]:
        copy.wait_recv()
    weights = [
        [all_near[c, pl.ds(quarter + chan * share + q, 1), :] for c in range(chans)] for q in range(share)
    ]
    for q in range(share):
        forms_ref[q, 0:quarter, :] = sum(weights[q][c] * all_near[c, 0:quarter, :] for c in range(chans))
    for copy in chan_copies[chans - 1 :]:
        copy.wait_recv()
    for q in range(share):
        forms_ref[q, quarter : 3 * quarter, :] = sum(weights[q][c] * all_far[c] for c in range(chans))


def image_kernel(local, scale, forms_ref, high_ref, left_ref, own_ref, power_ref, maps_ref, split):
    power_ref[0] = own_ref[...] * scale
    forms, _, both = forms_ref.shape
    quarter = both // 8
    columns = power_ref.shape[1]

    for f in range(forms):
        parts = [forms_ref[f, k * quarter : (k + 1) * quarter, :] for k in range(3)]
        high, low = symmetric(*parts, local)
        split[f * both : (f + 1) * both, 0:both] = high
        split[f * both : (f + 1) * both, both : 2 * both] = low

    for m in range(columns):
        high, left = high_ref[m], left_ref[m]
        right = jnp.dot(split[...], jnp.concatenate([high, high], axis=0), preferred_element_type=jnp.float32)
        for f in range(forms):
            line = jnp.sum(left * right[f * both : (f + 1) * both], axis=0, keepdims=True) * scale
            maps_ref[f, m : m + 1, :] = line


def on_device(voltages, kernels, footprint, cal_weight):
    local, _, _, samples = voltages.shape
    rows, chans = lax.axis_size("row"), lax.axis_size("chan")
    taps, maps = kernels.shape[2], cal_weight.shape[0]
    stations = local * rows
    both = 2 * stations
    share = maps // chans
    columns = GRID // rows
    scale = 1.0 / (2.0 * samples * stations * taps * taps)
    hbm = pl.BlockSpec(memory_space=pltpu.HBM)
    vmem = pl.BlockSpec(memory_space=pltpu.VMEM)
    f32 = jnp.float32
    forms, high, left, own = pl.pallas_call(
        functools.partial(gather_kernel, rows, chans),
        out_shape=(
            jax.ShapeDtypeStruct((share, 3 * stations // 4, both), f32),
            jax.ShapeDtypeStruct((columns, both, GRID), jnp.bfloat16),
            jax.ShapeDtypeStruct((columns, both, GRID), f32),
            jax.ShapeDtypeStruct((columns, GRID), f32),
        ),
        in_specs=[hbm] * 4,
        out_specs=(vmem,) * 4,
        scratch_shapes=[
            pltpu.VMEM((local, 2, samples), jnp.bfloat16),
            pltpu.VMEM((2, taps, local), f32),
            pltpu.VMEM((2, local), jnp.int32),
            pltpu.VMEM((1, maps), f32),
            pltpu.VMEM((LANES, LANES), f32),
            pltpu.VMEM((rows, local, LANES), f32),
            pltpu.VMEM((HALVES, 2 * local, samples // HALVES), jnp.bfloat16),
            pltpu.VMEM((rows, 2 * local, samples // HALVES), jnp.bfloat16),
            pltpu.VMEM((stations // 4, both), f32),
            pltpu.VMEM((stations // 4, both), f32),
            pltpu.VMEM((stations // 2, both), f32),
            pltpu.VMEM((stations // 2, both), f32),
            pltpu.VMEM((chans, stations // 4 + maps, both), f32),
            pltpu.VMEM((chans, stations // 2, both), f32),
            pltpu.VMEM((both, 2 * both), jnp.bfloat16),
            pltpu.SemaphoreType.DMA((4,)),
            pltpu.SemaphoreType.DMA((rows,)),
            pltpu.SemaphoreType.DMA((rows,)),
            pltpu.SemaphoreType.DMA((rows,)),
            pltpu.SemaphoreType.DMA((rows,)),
            pltpu.SemaphoreType.DMA((2,)),
            pltpu.SemaphoreType.DMA((2,)),
            pltpu.SemaphoreType.DMA((chans,)),
            pltpu.SemaphoreType.DMA((chans,)),
            pltpu.SemaphoreType.DMA((chans,)),
            pltpu.SemaphoreType.DMA((chans,)),
        ],
        compiler_params=pltpu.CompilerParams(
            collective_id=0, has_side_effects=True, vmem_limit_bytes=20 * 1024 * 1024
        ),
    )(*(
        pltpu.with_memory_space_constraint(x, pltpu.HBM)
        for x in (voltages[:, :, 0, :], jnp.transpose(kernels, (1, 2, 0)), footprint.T, cal_weight.T)
    ))
    power, cal_maps = pl.pallas_call(
        functools.partial(image_kernel, local, scale),
        out_shape=(
            jax.ShapeDtypeStruct((1, columns, GRID), f32),
            jax.ShapeDtypeStruct((share, columns, GRID), f32),
        ),
        in_specs=[vmem] * 4,
        out_specs=(vmem,) * 2,
        scratch_shapes=[pltpu.VMEM((share * both, 2 * both), jnp.bfloat16)],
        compiler_params=pltpu.CompilerParams(vmem_limit_bytes=20 * 1024 * 1024),
    )(forms, high, left, own)
    return jnp.swapaxes(power, 1, 2), jnp.swapaxes(cal_maps, 1, 2)


def solution(mesh):
    placed = (P("row", None, "chan", None), P("row", None, None), P("row", None), P(None, "chan"))
    return jax.shard_map(
        on_device,
        mesh=mesh,
        in_specs=placed,
        out_specs=(P("chan", None, "row"), P("chan", None, "row")),
        check_vma=False,
    )
```

```python
import functools
import math

import jax
import jax.numpy as jnp
from jax import lax
from jax.experimental import pallas as pl
from jax.experimental.pallas import tpu as pltpu
from jax.sharding import PartitionSpec as P

GRID = 256
HALVES = 2
LANES = 128
MESH = pl.DeviceIdType.MESH


def unit_circle(phase):
    turn = jnp.where(phase >= GRID // 2, phase - GRID, phase).astype(jnp.float32)
    half = turn * (math.pi / GRID)
    square = half * half
    sin_half = 0.0
    for order in (11, 9, 7, 5, 3, 1):
        sin_half = sin_half * square + (-1.0) ** (order // 2) / math.factorial(order)
    sin_half = sin_half * half
    cos_half = 0.0
    for order in (12, 10, 8, 6, 4, 2, 0):
        cos_half = cos_half * square + (-1.0) ** (order // 2) / math.factorial(order)
    return 1.0 - 2.0 * sin_half * sin_half, 2.0 * sin_half * cos_half


def response(weights, start, first, count):
    stations, taps = weights.shape
    place = first + lax.broadcasted_iota(jnp.int32, (stations, count), 1)
    base_real, base_imag = unit_circle((start * place) & (GRID - 1))
    step = lax.broadcasted_iota(jnp.int32, (8, count), 0)
    place = first + lax.broadcasted_iota(jnp.int32, (8, count), 1)
    tap_real, tap_imag = unit_circle((step * place) & (GRID - 1))
    sum_real, sum_imag = 0.0, 0.0
    for k in range(taps):
        weight = weights[:, k : k + 1]
        sum_real = sum_real + weight * tap_real[k : k + 1, :]
        sum_imag = sum_imag + weight * tap_imag[k : k + 1, :]
    return (
        base_real * sum_real - base_imag * sum_imag,
        base_real * sum_imag + base_imag * sum_real,
    )


def turned(values, local):
    lanes = values.shape[1]
    lane = lax.broadcasted_iota(jnp.int32, values.shape, 1)
    later = pltpu.roll(values, lanes - local, 1)
    earlier = pltpu.roll(values, local, 1)
    return jnp.where((lane // local) % 2 == 0, -later, earlier)


def laced(first, second, local):
    shape = (first.shape[0] // local, local, first.shape[1])
    both = jnp.stack([first.reshape(shape), second.reshape(shape)], axis=1)
    return both.reshape(2 * first.shape[0], first.shape[1])


def gather_kernel(
    rows, chans, volt_hbm, kern_hbm, foot_hbm, cal_hbm,
    forms_ref, high_ref, left_ref,
    volt, kern, foot, cal, fields, meta, halves, held, vis_near, vis_far,
    load, meta_send, meta_recv, volt_send, volt_recv, near_send, near_recv, far_send, far_recv,
):
    row, chan = lax.axis_index("row"), lax.axis_index("chan")
    local = volt.shape[0]
    width = halves.shape[2]
    maps, taps = cal.shape[1], kern.shape[1]
    twin = row + 1 - 2 * (row % 2)
    side = rows // 2
    mine_side, place = row // side, row % side
    row_peers = [(side, (1 - mine_side) * side + place)]
    for j in range(1, side):
        row_peers.append((j, mine_side * side + (place + j) % side))
        row_peers.append((side + j, (1 - mine_side) * side + (place + j) % side))
    slot = (row + mine_side * side) % rows
    vis_peers = [
        (2 * d + h, (chan + d) % chans, twin if h else row)
        for d in range(chans) for h in range(2) if d or h
    ]

    barrier = pltpu.get_barrier_semaphore()
    for _, peer in row_peers:
        pl.semaphore_signal(barrier, inc=1, device_id={"chan": chan, "row": peer}, device_id_type=MESH)
    for k, other, peer in vis_peers:
        if k != 1:
            pl.semaphore_signal(barrier, inc=1, device_id={"chan": other, "row": peer}, device_id_type=MESH)

    loads = [
        pltpu.make_async_copy(source, target, load.at[k])
        for k, (source, target) in enumerate(
            ((volt_hbm, volt), (kern_hbm, kern), (foot_hbm, foot), (cal_hbm, cal))
        )
    ]
    for copy in loads:
        copy.start()
    loads[0].wait()
    for h in range(HALVES):
        part = volt[:, :, h * width : (h + 1) * width].astype(jnp.float32)
        halves[h] = jnp.concatenate([part[:, 0, :], part[:, 1, :]], axis=0).astype(jnp.bfloat16)
    held[slot] = halves[row % 2]

    pl.semaphore_wait(barrier, len(row_peers) + len(vis_peers) - 1)

    volt_copies = []
    for k, peer in row_peers:
        volt_copies.append(pltpu.make_async_remote_copy(
            src_ref=halves.at[peer % 2], dst_ref=held.at[(row + peer // side * side) % rows],
            send_sem=volt_send.at[k], recv_sem=volt_recv.at[k],
            device_id={"chan": chan, "row": peer}, device_id_type=MESH,
        ))
        volt_copies[-1].start()

    fields[...] = jnp.zeros_like(fields)
    for copy in loads[1:]:
        copy.wait()
    fields[0:taps, 0:local] = kern[0]
    fields[taps : 2 * taps, 0:local] = kern[1]
    fields[2 * taps : 2 * taps + 2, 0:local] = foot[...].astype(jnp.float32)
    fields[2 * taps + 2 : 2 * taps + 3, 0:maps] = cal[...]
    turned_fields = fields[...].T
    meta[slot] = turned_fields[0:local, :]
    cal_column = turned_fields[0:maps, 2 * taps + 2 : 2 * taps + 3]
    copies = []
    for k, peer in row_peers:
        copies.append(pltpu.make_async_remote_copy(
            src_ref=meta.at[slot], dst_ref=meta.at[(row + peer // side * side) % rows],
            send_sem=meta_send.at[k], recv_sem=meta_recv.at[k],
            device_id={"chan": chan, "row": peer}, device_id_type=MESH,
        ))
        copies[-1].start()
    stations = rows * local
    both, quarter = 2 * stations, stations // 4
    mine = 2 * chan + row % 2

    def correlate(first, second):
        products = lax.dot_general(
            first, second, (((1,), (1,)), ((), ())), preferred_element_type=jnp.float32
        ).reshape(first.shape[0] // (2 * local), 2, local, both)
        count = first.shape[0] // 2
        return products[:, 0].reshape(count, both) - turned(products[:, 1].reshape(count, both), local)

    def exchange(buffer, send_sem, recv_sem):
        sends = []
        for k, other, peer in vis_peers:
            sends.append(pltpu.make_async_remote_copy(
                src_ref=buffer.at[mine], dst_ref=buffer.at[mine],
                send_sem=send_sem.at[k], recv_sem=recv_sem.at[k],
                device_id={"chan": other, "row": peer}, device_id_type=MESH,
            ))
            sends[-1].start()
        return sends

    left_lanes = lax.broadcasted_iota(jnp.int32, (quarter, both), 1) < stations
    for (k, _), copy in zip(row_peers, volt_copies):
        if k < side:
            copy.wait_recv()
    near = held[0:side].reshape(stations, width)
    seen = correlate(near, jnp.concatenate([near, near], axis=0))
    vis_near[mine, 0:quarter, :] = jnp.where(left_lanes, seen[:quarter], seen[quarter:])
    vis_near[mine, quarter : quarter + maps, :] = jnp.broadcast_to(cal_column, (maps, both))
    vis_copies = exchange(vis_near, near_send, near_recv)

    for (k, _), copy in zip(row_peers, volt_copies):
        if k >= side:
            copy.wait_recv()
    far = held[side:rows].reshape(stations, width)
    seen = correlate(jnp.concatenate([near, far], axis=0), jnp.concatenate([far, far], axis=0))
    for part in range(2):
        lo = 2 * part * quarter
        vis_far[mine, part * quarter : (part + 1) * quarter, :] = jnp.where(
            left_lanes, seen[lo : lo + quarter], seen[lo + quarter : lo + 2 * quarter]
        )
    vis_copies += exchange(vis_far, far_send, far_recv)
    for copy in copies:
        copy.wait()
    known = meta[...].reshape(stations, LANES)
    starts = known[:, 2 * taps : 2 * taps + 2].astype(jnp.int32)
    a_real, a_imag = response(known[:, 0:taps], starts[:, 0:1], 0, GRID)
    b_real, b_imag = response(known[:, taps : 2 * taps], starts[:, 1:2], row * (GRID // rows), LANES)
    columns = left_ref.shape[0]
    group = min(columns, 4)

    def steer(step, carry):
        b_real, b_imag = carry
        for j in range(group):
            one_real, one_imag = b_real[:, j : j + 1], b_imag[:, j : j + 1]
            whole = laced(a_real * one_real - a_imag * one_imag, a_real * one_imag + a_imag * one_real, local)
            high = whole.astype(jnp.bfloat16)
            high_ref[step * group + j] = high
            left_ref[step * group + j] = 2.0 * whole - high.astype(jnp.float32)
        return pltpu.roll(b_real, LANES - group, 1), pltpu.roll(b_imag, LANES - group, 1)

    lax.fori_loop(0, columns // group, steer, (b_real, b_imag))

    for copy in volt_copies + vis_copies:
        copy.wait_send()

    share = maps // chans
    for copy in vis_copies[: len(vis_peers)]:
        copy.wait_recv()
    weights = [
        [vis_near[2 * c, pl.ds(quarter + chan * share + q, 1), :] for c in range(chans)] for q in range(share)
    ]
    near_total = [vis_near[2 * c, 0:quarter, :] + vis_near[2 * c + 1, 0:quarter, :] for c in range(chans)]
    forms_ref[0, 0:quarter, :] = vis_near[2 * chan, 0:quarter, :] + vis_near[2 * chan + 1, 0:quarter, :]
    for q in range(share):
        forms_ref[1 + q, 0:quarter, :] = sum(weights[q][c] * near_total[c] for c in range(chans))
    for copy in vis_copies[len(vis_peers) :]:
        copy.wait_recv()
    far_total = [vis_far[2 * c] + vis_far[2 * c + 1] for c in range(chans)]
    forms_ref[0, quarter : 3 * quarter, :] = vis_far[2 * chan] + vis_far[2 * chan + 1]
    for q in range(share):
        forms_ref[1 + q, quarter : 3 * quarter, :] = sum(weights[q][c] * far_total[c] for c in range(chans))


def image_kernel(local, scale, forms_ref, high_ref, left_ref, power_ref, maps_ref, split):
    forms, _, both = forms_ref.shape
    stations, quarter = both // 2, both // 8
    columns = power_ref.shape[1]

    for f in range(forms):
        left_lanes = lax.broadcasted_iota(jnp.int32, (quarter, both), 1) < stations
        near, cross, far = (forms_ref[f, k * quarter : (k + 1) * quarter, :] for k in range(3))
        near, far = 0.5 * near, 0.5 * far
        top = jnp.concatenate([
            jnp.where(left_lanes, near, pltpu.roll(cross, stations, 1)),
            jnp.where(left_lanes, pltpu.roll(near, stations, 1), cross),
            jnp.where(left_lanes, 0.0, pltpu.roll(far, stations, 1)),
            jnp.where(left_lanes, 0.0, far),
        ], axis=0)
        whole = laced(top, turned(top, local), local)
        whole = whole + whole.T
        high = whole.astype(jnp.bfloat16)
        split[f * both : (f + 1) * both, 0:both] = high
        split[f * both : (f + 1) * both, both : 2 * both] = (whole - high.astype(jnp.float32)).astype(jnp.bfloat16)

    for m in range(columns):
        high, left = high_ref[m], left_ref[m]
        right = jnp.dot(split[...], jnp.concatenate([high, high], axis=0), preferred_element_type=jnp.float32)
        for f in range(forms):
            line = jnp.sum(left * right[f * both : (f + 1) * both], axis=0, keepdims=True) * scale
            if f == 0:
                power_ref[0, m : m + 1, :] = line
            else:
                maps_ref[f - 1, m : m + 1, :] = line


def on_device(voltages, kernels, footprint, cal_weight):
    local, _, _, samples = voltages.shape
    rows, chans = lax.axis_size("row"), lax.axis_size("chan")
    taps, maps = kernels.shape[2], cal_weight.shape[0]
    stations = local * rows
    both = 2 * stations
    share = maps // chans
    columns = GRID // rows
    scale = 1.0 / (2.0 * samples * stations * taps * taps)
    hbm = pl.BlockSpec(memory_space=pltpu.HBM)
    vmem = pl.BlockSpec(memory_space=pltpu.VMEM)
    f32 = jnp.float32
    forms, high, left = pl.pallas_call(
        functools.partial(gather_kernel, rows, chans),
        out_shape=(
            jax.ShapeDtypeStruct((1 + share, 3 * stations // 4, both), f32),
            jax.ShapeDtypeStruct((columns, both, GRID), jnp.bfloat16),
            jax.ShapeDtypeStruct((columns, both, GRID), f32),
        ),
        in_specs=[hbm] * 4,
        out_specs=(vmem,) * 3,
        scratch_shapes=[
            pltpu.VMEM((local, 2, samples), jnp.bfloat16),
            pltpu.VMEM((2, taps, local), f32),
            pltpu.VMEM((2, local), jnp.int32),
            pltpu.VMEM((1, maps), f32),
            pltpu.VMEM((LANES, LANES), f32),
            pltpu.VMEM((rows, local, LANES), f32),
            pltpu.VMEM((HALVES, 2 * local, samples // HALVES), jnp.bfloat16),
            pltpu.VMEM((rows, 2 * local, samples // HALVES), jnp.bfloat16),
            pltpu.VMEM((2 * chans, stations // 4 + maps, both), f32),
            pltpu.VMEM((2 * chans, stations // 2, both), f32),
            pltpu.SemaphoreType.DMA((4,)),
            pltpu.SemaphoreType.DMA((rows,)),
            pltpu.SemaphoreType.DMA((rows,)),
            pltpu.SemaphoreType.DMA((rows,)),
            pltpu.SemaphoreType.DMA((rows,)),
            pltpu.SemaphoreType.DMA((2 * chans,)),
            pltpu.SemaphoreType.DMA((2 * chans,)),
            pltpu.SemaphoreType.DMA((2 * chans,)),
            pltpu.SemaphoreType.DMA((2 * chans,)),
        ],
        compiler_params=pltpu.CompilerParams(
            collective_id=0, has_side_effects=True, vmem_limit_bytes=20 * 1024 * 1024
        ),
    )(*(
        pltpu.with_memory_space_constraint(x, pltpu.HBM)
        for x in (voltages[:, :, 0, :], jnp.transpose(kernels, (1, 2, 0)), footprint.T, cal_weight.T)
    ))
    power, cal_maps = pl.pallas_call(
        functools.partial(image_kernel, local, scale),
        out_shape=(
            jax.ShapeDtypeStruct((1, columns, GRID), f32),
            jax.ShapeDtypeStruct((share, columns, GRID), f32),
        ),
        in_specs=[vmem] * 3,
        out_specs=(vmem,) * 2,
        scratch_shapes=[pltpu.VMEM(((1 + share) * both, 2 * both), jnp.bfloat16)],
        compiler_params=pltpu.CompilerParams(vmem_limit_bytes=20 * 1024 * 1024),
    )(forms, high, left)
    return jnp.swapaxes(power, 1, 2), jnp.swapaxes(cal_maps, 1, 2)


def solution(mesh):
    placed = (P("row", None, "chan", None), P("row", None, None), P("row", None), P(None, "chan"))
    return jax.shard_map(
        on_device,
        mesh=mesh,
        in_specs=placed,
        out_specs=(P("chan", None, "row"), P("chan", None, "row")),
        check_vma=False,
    )
```

```python
import functools
import math

import jax
import jax.numpy as jnp
from jax import lax
from jax.experimental import pallas as pl
from jax.experimental.pallas import tpu as pltpu
from jax.sharding import PartitionSpec as P

GRID = 256
HALVES = 2
LANES = 128
MESH = pl.DeviceIdType.MESH


def unit_circle(phase):
    turn = jnp.where(phase >= GRID // 2, phase - GRID, phase).astype(jnp.float32)
    half = turn * (math.pi / GRID)
    square = half * half
    sin_half = 0.0
    for order in (11, 9, 7, 5, 3, 1):
        sin_half = sin_half * square + (-1.0) ** (order // 2) / math.factorial(order)
    sin_half = sin_half * half
    cos_half = 0.0
    for order in (12, 10, 8, 6, 4, 2, 0):
        cos_half = cos_half * square + (-1.0) ** (order // 2) / math.factorial(order)
    return 1.0 - 2.0 * sin_half * sin_half, 2.0 * sin_half * cos_half


def response(weights, start, first, count):
    stations, taps = weights.shape
    place = first + lax.broadcasted_iota(jnp.int32, (stations, count), 1)
    base_real, base_imag = unit_circle((start * place) & (GRID - 1))
    step = lax.broadcasted_iota(jnp.int32, (8, count), 0)
    place = first + lax.broadcasted_iota(jnp.int32, (8, count), 1)
    tap_real, tap_imag = unit_circle((step * place) & (GRID - 1))
    sum_real, sum_imag = 0.0, 0.0
    for k in range(taps):
        weight = weights[:, k : k + 1]
        sum_real = sum_real + weight * tap_real[k : k + 1, :]
        sum_imag = sum_imag + weight * tap_imag[k : k + 1, :]
    return (
        base_real * sum_real - base_imag * sum_imag,
        base_real * sum_imag + base_imag * sum_real,
    )


def turned(values, local):
    lanes = values.shape[1]
    lane = lax.broadcasted_iota(jnp.int32, values.shape, 1)
    later = pltpu.roll(values, lanes - local, 1)
    earlier = pltpu.roll(values, local, 1)
    return jnp.where((lane // local) % 2 == 0, -later, earlier)


def laced(first, second, local):
    shape = (first.shape[0] // local, local, first.shape[1])
    both = jnp.stack([first.reshape(shape), second.reshape(shape)], axis=1)
    return both.reshape(2 * first.shape[0], first.shape[1])


def gather_kernel(
    rows, chans, volt_hbm, kern_hbm, foot_hbm, cal_hbm,
    forms_ref, high_ref, left_ref,
    volt, kern, foot, cal, fields, meta, halves, held, vis_near, vis_far,
    load, meta_send, meta_recv, volt_send, volt_recv, near_send, near_recv, far_send, far_recv,
):
    row, chan = lax.axis_index("row"), lax.axis_index("chan")
    local = volt.shape[0]
    width = halves.shape[2]
    maps, taps = cal.shape[1], kern.shape[1]
    twin = row + 1 - 2 * (row % 2)
    side = rows // 2
    mine_side, place = row // side, row % side
    row_peers = [(side, (1 - mine_side) * side + place)]
    for j in range(1, side):
        row_peers.append((j, mine_side * side + (place + j) % side))
        row_peers.append((side + j, (1 - mine_side) * side + (place + j) % side))
    slot = (row + mine_side * side) % rows
    vis_peers = [
        (2 * d + h, (chan + d) % chans, twin if h else row)
        for d, h in [(d, h) for h in (1, 0) for d in range(1, chans)] + [(0, 1)]
    ]

    barrier = pltpu.get_barrier_semaphore()
    for _, peer in row_peers:
        pl.semaphore_signal(barrier, inc=1, device_id={"chan": chan, "row": peer}, device_id_type=MESH)
    for k, other, peer in vis_peers:
        if k != 1:
            pl.semaphore_signal(barrier, inc=1, device_id={"chan": other, "row": peer}, device_id_type=MESH)

    loads = [
        pltpu.make_async_copy(source, target, load.at[k])
        for k, (source, target) in enumerate(
            ((volt_hbm, volt), (kern_hbm, kern), (foot_hbm, foot), (cal_hbm, cal))
        )
    ]
    for copy in loads:
        copy.start()
    loads[0].wait()
    for h in range(HALVES):
        part = volt[:, :, h * width : (h + 1) * width].astype(jnp.float32)
        halves[h] = jnp.concatenate([part[:, 0, :], part[:, 1, :]], axis=0).astype(jnp.bfloat16)
    held[slot] = halves[row % 2]

    pl.semaphore_wait(barrier, len(row_peers) + len(vis_peers) - 1)

    volt_copies = []
    for k, peer in row_peers:
        volt_copies.append(pltpu.make_async_remote_copy(
            src_ref=halves.at[peer % 2], dst_ref=held.at[(row + peer // side * side) % rows],
            send_sem=volt_send.at[k], recv_sem=volt_recv.at[k],
            device_id={"chan": chan, "row": peer}, device_id_type=MESH,
        ))
        volt_copies[-1].start()

    fields[...] = jnp.zeros_like(fields)
    for copy in loads[1:]:
        copy.wait()
    fields[0:taps, 0:local] = kern[0]
    fields[taps : 2 * taps, 0:local] = kern[1]
    fields[2 * taps : 2 * taps + 2, 0:local] = foot[...].astype(jnp.float32)
    fields[2 * taps + 2 : 2 * taps + 3, 0:maps] = cal[...]
    turned_fields = fields[...].T
    meta[slot] = turned_fields[0:local, :]
    cal_column = turned_fields[0:maps, 2 * taps + 2 : 2 * taps + 3]
    copies = []
    for k, peer in row_peers:
        copies.append(pltpu.make_async_remote_copy(
            src_ref=meta.at[slot], dst_ref=meta.at[(row + peer // side * side) % rows],
            send_sem=meta_send.at[k], recv_sem=meta_recv.at[k],
            device_id={"chan": chan, "row": peer}, device_id_type=MESH,
        ))
        copies[-1].start()
    stations = rows * local
    both, quarter = 2 * stations, stations // 4
    mine = 2 * chan + row % 2

    def correlate(first, second):
        products = lax.dot_general(
            first, second, (((1,), (1,)), ((), ())), preferred_element_type=jnp.float32
        ).reshape(first.shape[0] // (2 * local), 2, local, both)
        count = first.shape[0] // 2
        return products[:, 0].reshape(count, both) - turned(products[:, 1].reshape(count, both), local)

    def exchange(buffer, send_sem, recv_sem):
        sends = []
        for k, other, peer in vis_peers:
            sends.append(pltpu.make_async_remote_copy(
                src_ref=buffer.at[mine], dst_ref=buffer.at[mine],
                send_sem=send_sem.at[k], recv_sem=recv_sem.at[k],
                device_id={"chan": other, "row": peer}, device_id_type=MESH,
            ))
            sends[-1].start()
        return sends

    left_lanes = lax.broadcasted_iota(jnp.int32, (quarter, both), 1) < stations
    for (k, _), copy in zip(row_peers, volt_copies):
        if k < side:
            copy.wait_recv()
    near = held[0:side].reshape(stations, width)
    seen = correlate(near, jnp.concatenate([near, near], axis=0))
    vis_near[mine, 0:quarter, :] = jnp.where(left_lanes, seen[:quarter], seen[quarter:])
    vis_near[mine, quarter : quarter + maps, :] = jnp.broadcast_to(cal_column, (maps, both))
    vis_copies = exchange(vis_near, near_send, near_recv)

    for (k, _), copy in zip(row_peers, volt_copies):
        if k >= side:
            copy.wait_recv()
    far = held[side:rows].reshape(stations, width)
    seen = correlate(jnp.concatenate([near, far], axis=0), jnp.concatenate([far, far], axis=0))
    for part in range(2):
        lo = 2 * part * quarter
        vis_far[mine, part * quarter : (part + 1) * quarter, :] = jnp.where(
            left_lanes, seen[lo : lo + quarter], seen[lo + quarter : lo + 2 * quarter]
        )
    vis_copies += exchange(vis_far, far_send, far_recv)
    for copy in copies:
        copy.wait()
    known = meta[...].reshape(stations, LANES)
    starts = known[:, 2 * taps : 2 * taps + 2].astype(jnp.int32)
    a_real, a_imag = response(known[:, 0:taps], starts[:, 0:1], 0, GRID)
    b_real, b_imag = response(known[:, taps : 2 * taps], starts[:, 1:2], row * (GRID // rows), LANES)
    columns = left_ref.shape[0]
    group = min(columns, 4)

    def steer(step, carry):
        b_real, b_imag = carry
        for j in range(group):
            one_real, one_imag = b_real[:, j : j + 1], b_imag[:, j : j + 1]
            whole = laced(a_real * one_real - a_imag * one_imag, a_real * one_imag + a_imag * one_real, local)
            high = whole.astype(jnp.bfloat16)
            high_ref[step * group + j] = high
            left_ref[step * group + j] = 2.0 * whole - high.astype(jnp.float32)
        return pltpu.roll(b_real, LANES - group, 1), pltpu.roll(b_imag, LANES - group, 1)

    lax.fori_loop(0, columns // group, steer, (b_real, b_imag))

    for copy in volt_copies + vis_copies:
        copy.wait_send()

    share = maps // chans
    for copy in vis_copies[: len(vis_peers)]:
        copy.wait_recv()
    weights = [
        [vis_near[2 * c, pl.ds(quarter + chan * share + q, 1), :] for c in range(chans)] for q in range(share)
    ]
    near_total = [vis_near[2 * c, 0:quarter, :] + vis_near[2 * c + 1, 0:quarter, :] for c in range(chans)]
    forms_ref[0, 0:quarter, :] = vis_near[2 * chan, 0:quarter, :] + vis_near[2 * chan + 1, 0:quarter, :]
    for q in range(share):
        forms_ref[1 + q, 0:quarter, :] = sum(weights[q][c] * near_total[c] for c in range(chans))
    for copy in vis_copies[len(vis_peers) :]:
        copy.wait_recv()
    far_total = [vis_far[2 * c] + vis_far[2 * c + 1] for c in range(chans)]
    forms_ref[0, quarter : 3 * quarter, :] = vis_far[2 * chan] + vis_far[2 * chan + 1]
    for q in range(share):
        forms_ref[1 + q, quarter : 3 * quarter, :] = sum(weights[q][c] * far_total[c] for c in range(chans))


def image_kernel(local, scale, forms_ref, high_ref, left_ref, power_ref, maps_ref, split):
    forms, _, both = forms_ref.shape
    stations, quarter = both // 2, both // 8
    columns = power_ref.shape[1]

    for f in range(forms):
        left_lanes = lax.broadcasted_iota(jnp.int32, (quarter, both), 1) < stations
        near, cross, far = (forms_ref[f, k * quarter : (k + 1) * quarter, :] for k in range(3))
        near, far = 0.5 * near, 0.5 * far
        top = jnp.concatenate([
            jnp.where(left_lanes, near, pltpu.roll(cross, stations, 1)),
            jnp.where(left_lanes, pltpu.roll(near, stations, 1), cross),
            jnp.where(left_lanes, 0.0, pltpu.roll(far, stations, 1)),
            jnp.where(left_lanes, 0.0, far),
        ], axis=0)
        whole = laced(top, turned(top, local), local)
        whole = whole + whole.T
        high = whole.astype(jnp.bfloat16)
        split[f * both : (f + 1) * both, 0:both] = high
        split[f * both : (f + 1) * both, both : 2 * both] = (whole - high.astype(jnp.float32)).astype(jnp.bfloat16)

    for m in range(columns):
        high, left = high_ref[m], left_ref[m]
        right = jnp.dot(split[...], jnp.concatenate([high, high], axis=0), preferred_element_type=jnp.float32)
        for f in range(forms):
            line = jnp.sum(left * right[f * both : (f + 1) * both], axis=0, keepdims=True) * scale
            if f == 0:
                power_ref[0, m : m + 1, :] = line
            else:
                maps_ref[f - 1, m : m + 1, :] = line


def on_device(voltages, kernels, footprint, cal_weight):
    local, _, _, samples = voltages.shape
    rows, chans = lax.axis_size("row"), lax.axis_size("chan")
    taps, maps = kernels.shape[2], cal_weight.shape[0]
    stations = local * rows
    both = 2 * stations
    share = maps // chans
    columns = GRID // rows
    scale = 1.0 / (2.0 * samples * stations * taps * taps)
    hbm = pl.BlockSpec(memory_space=pltpu.HBM)
    vmem = pl.BlockSpec(memory_space=pltpu.VMEM)
    f32 = jnp.float32
    forms, high, left = pl.pallas_call(
        functools.partial(gather_kernel, rows, chans),
        out_shape=(
            jax.ShapeDtypeStruct((1 + share, 3 * stations // 4, both), f32),
            jax.ShapeDtypeStruct((columns, both, GRID), jnp.bfloat16),
            jax.ShapeDtypeStruct((columns, both, GRID), f32),
        ),
        in_specs=[hbm] * 4,
        out_specs=(vmem,) * 3,
        scratch_shapes=[
            pltpu.VMEM((local, 2, samples), jnp.bfloat16),
            pltpu.VMEM((2, taps, local), f32),
            pltpu.VMEM((2, local), jnp.int32),
            pltpu.VMEM((1, maps), f32),
            pltpu.VMEM((LANES, LANES), f32),
            pltpu.VMEM((rows, local, LANES), f32),
            pltpu.VMEM((HALVES, 2 * local, samples // HALVES), jnp.bfloat16),
            pltpu.VMEM((rows, 2 * local, samples // HALVES), jnp.bfloat16),
            pltpu.VMEM((2 * chans, stations // 4 + maps, both), f32),
            pltpu.VMEM((2 * chans, stations // 2, both), f32),
            pltpu.SemaphoreType.DMA((4,)),
            pltpu.SemaphoreType.DMA((rows,)),
            pltpu.SemaphoreType.DMA((rows,)),
            pltpu.SemaphoreType.DMA((rows,)),
            pltpu.SemaphoreType.DMA((rows,)),
            pltpu.SemaphoreType.DMA((2 * chans,)),
            pltpu.SemaphoreType.DMA((2 * chans,)),
            pltpu.SemaphoreType.DMA((2 * chans,)),
            pltpu.SemaphoreType.DMA((2 * chans,)),
        ],
        compiler_params=pltpu.CompilerParams(
            collective_id=0, has_side_effects=True, vmem_limit_bytes=20 * 1024 * 1024
        ),
    )(*(
        pltpu.with_memory_space_constraint(x, pltpu.HBM)
        for x in (voltages[:, :, 0, :], jnp.transpose(kernels, (1, 2, 0)), footprint.T, cal_weight.T)
    ))
    power, cal_maps = pl.pallas_call(
        functools.partial(image_kernel, local, scale),
        out_shape=(
            jax.ShapeDtypeStruct((1, columns, GRID), f32),
            jax.ShapeDtypeStruct((share, columns, GRID), f32),
        ),
        in_specs=[vmem] * 3,
        out_specs=(vmem,) * 2,
        scratch_shapes=[pltpu.VMEM(((1 + share) * both, 2 * both), jnp.bfloat16)],
        compiler_params=pltpu.CompilerParams(vmem_limit_bytes=20 * 1024 * 1024),
    )(forms, high, left)
    return jnp.swapaxes(power, 1, 2), jnp.swapaxes(cal_maps, 1, 2)


def solution(mesh):
    placed = (P("row", None, "chan", None), P("row", None, None), P("row", None), P(None, "chan"))
    return jax.shard_map(
        on_device,
        mesh=mesh,
        in_specs=placed,
        out_specs=(P("chan", None, "row"), P("chan", None, "row")),
        check_vma=False,
    )
```
